32 devices in a mesh: member: 2 (over core), fsdp: 16 (over z, y, x).
Axes of the slice: x: 2, y: 2, z: 4, core: 2. Of those that a mesh axis runs over, the one named last changes fastest.
Arguments:
- hidden: bfloat16 [2, 512, 2048], P('member', 'fsdp'), may hold values from -60 to 60
- gain: float32 [2, 2048], P('member'), may hold values from 0.5 to 1.5
- head: bfloat16 [2, 2048, 128256], P('member', None, 'fsdp'), may hold values from -0.397747564 to 0.397747564
- labels: int32 [512], replicated, may hold values from 0 to 128255
Outputs:
- token_loss: float32 [2, 512], P('member', 'fsdp')
- head_grad: bfloat16 [2, 2048, 128256], P('member', None, 'fsdp')
- hidden_grad: bfloat16 [2, 512, 2048], P('member', 'fsdp')
The draws below stay inside these ranges and needn't reach their ends.
All inputs are finite; a program needn't handle non-finite values.
Results may differ from the reference program's by a relative error of at most 0.0049.
Values may be sent and summed in bfloat16 or wider, within the bound.
No kernel may reach another device: no remote copies, remote signals or barrier semaphores. Data moves between devices by JAX's collectives and lax.ppermute only.
A program may use at most 128 MiB of HBM per device.

```python
import math
import jax
import jax.numpy as jnp
from jax import lax

D = 2048
VOCAB = 128256
TOKENS = 512
MEMBERS = 2


def draw_hidden(key, part):
    values = jax.random.normal(jax.random.fold_in(key, 1), (MEMBERS, TOKENS, D), jnp.float32)
    values = jnp.clip(values, -6.0, 6.0)
    return values.astype(jnp.bfloat16)


def draw_head(key, part):
    values = jax.random.normal(jax.random.fold_in(key, 3), (MEMBERS, D, VOCAB), jnp.float32)
    values = jnp.clip(values, -6.0, 6.0) * (3.0 / math.sqrt(D))
    return values.astype(jnp.bfloat16)


def set_ends(drawn, rng, low, high):
    longest = drawn.shape.index(max(drawn.shape))
    spots = []
    for shift in (0, 1):
        where = [jax.random.randint(jax.random.fold_in(rng, axis), (), 0, length) for axis, length in enumerate(drawn.shape)]
        where[longest] = (where[longest] + shift) % drawn.shape[longest]
        spots.append(tuple(where))
    return drawn.at[spots[0]].set(low).at[spots[1]].set(high)


def setup_inputs(seed: int = 0) -> dict:
    keys = jax.random.split(jax.random.key(seed), 5)
    hidden = draw_hidden(jax.random.fold_in(keys[4], 71), 0)
    gain = jnp.clip(1.0 + 0.1 * jax.random.normal(keys[1], (MEMBERS, D), jnp.float32), 0.5, 1.5)
    head = draw_head(jax.random.fold_in(keys[4], 71), 0)
    labels = set_ends(jax.random.randint(keys[3], (TOKENS,), 0, VOCAB), jax.random.fold_in(keys[3], 1), 0, VOCAB - 1).astype(jnp.int32)
    return dict(hidden=hidden, gain=gain, head=head, labels=labels)


EPS = 1e-05
BETA = 0.5

def normalize(rows, gain_row):
    values = rows.astype(jnp.float32)
    inverse = lax.rsqrt(lax.optimization_barrier(jnp.mean(values * values, axis=-1, keepdims=True)) + EPS)
    return ((values * inverse * gain_row).astype(jnp.bfloat16), inverse)

def norm_back(rows, inverse, gain_row, upstream):
    values = rows.astype(jnp.float32)
    scaled = gain_row * upstream
    inner = lax.optimization_barrier(jnp.mean(scaled * values, axis=-1, keepdims=True))
    return inverse * scaled - values * inverse ** 3 * inner

def reference(hidden, gain, head, labels):
    normed_list = []
    inverse_list = []
    logit_list = []
    total_list = []
    logprob_list = []
    for member in range(MEMBERS):
        normed, inverse = normalize(hidden[member], gain[member])
        logits = jnp.dot(normed, head[member], preferred_element_type=jnp.float32)
        row_top = lax.optimization_barrier(jnp.max(logits, axis=-1))
        row_total = lax.optimization_barrier(jnp.sum(jnp.exp(logits - row_top[:, None]), axis=-1))
        log_total = row_top + jnp.log(row_total)
        normed_list.append(normed)
        inverse_list.append(inverse)
        logit_list.append(logits)
        total_list.append(log_total)
        logprob_list.append((logits - log_total[:, None]).astype(jnp.bfloat16))
    columns = jnp.arange(VOCAB, dtype=jnp.int32)
    onehot = (labels[:, None] == columns[None, :]).astype(jnp.float32)
    losses = []
    head_grads = []
    hidden_grads = []
    for member in range(MEMBERS):
        logits = logit_list[member]
        log_total = total_list[member]
        target = jnp.exp(logprob_list[member ^ 1].astype(jnp.float32))
        student = jnp.exp(logits - log_total[:, None])
        dlogits = (((1.0 + BETA) * student - onehot - BETA * target) / TOKENS).astype(jnp.bfloat16)
        picked = lax.optimization_barrier(jnp.sum(onehot * logits, axis=-1))
        cross = lax.optimization_barrier(jnp.sum(target * (log_total[:, None] - logits), axis=-1))
        losses.append(log_total - picked + BETA * cross)
        head_grads.append(jnp.dot(normed_list[member].T, dlogits, preferred_element_type=jnp.float32).astype(jnp.bfloat16))
        upstream = jnp.dot(dlogits, head[member].T, preferred_element_type=jnp.float32)
        hidden_grads.append(norm_back(hidden[member], inverse_list[member], gain[member], upstream).astype(jnp.bfloat16))
    return (jnp.stack(losses), jnp.stack(head_grads), jnp.stack(hidden_grads))
```

```python
import functools
import jax
import jax.numpy as jnp
from jax import lax
from jax.experimental import pallas as pl
from jax.experimental.pallas import tpu as pltpu
from jax.sharding import PartitionSpec as P

EPS = 1e-05
BETA = 0.5
TILE = 1024
CHUNK = 128
LANES = 128
VMEM_LIMIT = 56 * 1024 * 1024


def cdiv(a, b):
    return -(-a // b)


def flip_bit(value, axis_name, bit):
    n = lax.axis_size(axis_name)
    return lax.ppermute(value, axis_name, [(i, i ^ (1 << bit)) for i in range(n)])


def tiling(vocab_dev):
    tile = min(TILE, cdiv(vocab_dev, 16) * 16)
    return tile, cdiv(vocab_dev, tile)


def whole(shape):
    return pl.BlockSpec(shape, lambda j: (0, 0))


def chunks(valid):
    return [
        (start, min(CHUNK, cdiv(valid - start, 16) * 16), min(CHUNK, valid - start))
        for start in range(0, valid, CHUNK)
    ]


def pick_row(table, index):
    here = lax.broadcasted_iota(jnp.int32, table.shape, 0) == index
    return jnp.sum(jnp.where(here, table, 0.0), axis=0, keepdims=True)


def logits_kernel(
    vocab_dev, tile, tiles, hidden_ref, gain_ref, labels_ref, w_ref,
    p_ref, l_ref, normed_ref, m_ref, stats_ref, logits_ref, s_ref, picked_ref,
):
    step = pl.program_id(0)
    tokens = hidden_ref.shape[0]

    def matmul(slot):
        logits_ref[slot] = lax.dot_general(
            w_ref[...], normed_ref[...], (((1,), (1,)), ((), ())), preferred_element_type=jnp.float32
        )

    def soften(slot, index, valid_rows):
        group = min(tokens, LANES)
        for col in range(0, tokens, group):
            cols = slice(col, col + group)
            target = labels_ref[:, cols] - index * tile
            top = None
            for start, rows, valid in chunks(valid_rows):
                values = logits_ref[slot, start : start + valid, cols]
                part = jnp.max(values, axis=0, keepdims=True)
                top = part if top is None else jnp.maximum(top, part)
            total = jnp.zeros((1, group), jnp.float32)
            picked = picked_ref[:, cols]
            for start, rows, valid in chunks(valid_rows):
                values = logits_ref[slot, start : start + rows, cols]
                row = lax.broadcasted_iota(jnp.int32, (rows, group), 0)
                lowered = values - top
                exps = jnp.exp(lowered)
                l_ref[start : start + rows, cols] = lowered.astype(l_ref.dtype)
                p_ref[start : start + rows, cols] = exps.astype(p_ref.dtype)
                chosen = jnp.where(row == target - start, values, 0.0)
                if valid < rows:
                    exps = jnp.where(row < valid, exps, 0.0)
                    chosen = jnp.where(row < valid, chosen, 0.0)
                total = total + jnp.sum(exps, axis=0, keepdims=True)
                picked = picked + jnp.sum(chosen, axis=0, keepdims=True)
            here = lax.broadcasted_iota(jnp.int32, (m_ref.shape[0], group), 0) == index
            m_ref[:, cols] = jnp.where(here, top, m_ref[:, cols])
            s_ref[:, cols] = jnp.where(here, total, s_ref[:, cols])
            picked_ref[:, cols] = picked

    @pl.when(step == 0)
    def _():
        for row in range(0, tokens, CHUNK):
            rows = slice(row, row + CHUNK)
            values = hidden_ref[rows, :].astype(jnp.float32)
            inverse = lax.rsqrt(jnp.mean(values * values, axis=-1, keepdims=True) + EPS)
            normed_ref[rows, :] = (values * inverse * gain_ref[...]).astype(jnp.bfloat16)
        m_ref[...] = jnp.full_like(m_ref, -jnp.inf)
        s_ref[...] = jnp.zeros_like(s_ref)
        picked_ref[...] = jnp.zeros_like(picked_ref)
        matmul(0)

    if tiles > 1:

        @pl.when((step > 0) & (step < tiles))
        def _():
            matmul(lax.rem(step, 2))
            soften(lax.rem(step + 1, 2), step - 1, tile)

    @pl.when(step == tiles)
    def _():
        soften((tiles - 1) % 2, tiles - 1, vocab_dev - (tiles - 1) * tile)
        tops = m_ref[...]
        top = jnp.max(tops, axis=0, keepdims=True)
        total = jnp.sum(s_ref[...] * jnp.exp(tops - top), axis=0, keepdims=True)
        stats_ref[...] = jnp.zeros_like(stats_ref)
        stats_ref[0:1, :] = top
        stats_ref[1:2, :] = total
        stats_ref[2:3, :] = picked_ref[...]


def run_logits(hidden, gain, labels, weights):
    tokens, width = hidden.shape
    vocab_dev = weights.shape[0]
    tile, tiles = tiling(vocab_dev)
    groups = cdiv(tiles, 8) * 8
    behind = pl.BlockSpec((tile, tokens), lambda j: (jnp.maximum(j - 1, 0), 0))
    return pl.pallas_call(
        functools.partial(logits_kernel, vocab_dev, tile, tiles),
        grid=(tiles + 1,),
        in_specs=[
            whole((tokens, width)),
            whole((1, width)),
            whole((1, tokens)),
            pl.BlockSpec((tile, width), lambda j: (jnp.minimum(j, tiles - 1), 0)),
        ],
        out_specs=[behind, behind, whole((tokens, width)), whole((groups, tokens)), whole((8, tokens))],
        out_shape=[
            jax.ShapeDtypeStruct((vocab_dev, tokens), jnp.bfloat16),
            jax.ShapeDtypeStruct((vocab_dev, tokens), jnp.bfloat16),
            jax.ShapeDtypeStruct((tokens, width), jnp.bfloat16),
            jax.ShapeDtypeStruct((groups, tokens), jnp.float32),
            jax.ShapeDtypeStruct((8, tokens), jnp.float32),
        ],
        scratch_shapes=[
            pltpu.VMEM((2, tile, tokens), jnp.float32),
            pltpu.VMEM((groups, tokens), jnp.float32),
            pltpu.VMEM((1, tokens), jnp.float32),
        ],
        compiler_params=pltpu.CompilerParams(vmem_limit_bytes=VMEM_LIMIT),
        cost_estimate=pl.CostEstimate(
            flops=2 * tokens * width * vocab_dev,
            bytes_accessed=2 * width * vocab_dev + 4 * tokens * vocab_dev,
            transcendentals=tokens * vocab_dev,
        ),
        name="logits",
    )(hidden, gain, labels, weights)


def dlogits_kernel(
    vocab_dev, tile, tiles, totals_ref, labels_ref, ms_ref, mt_ref, ps_ref, pt_ref, l_ref, w_ref,
    d_ref, up_ref, cross_ref, d_scratch, a_ref, b_ref, g_ref, c_ref,
):
    step = pl.program_id(0)
    tokens = ps_ref.shape[1]
    scale = 1.0 / tokens
    last_rows = vocab_dev - (tiles - 1) * tile

    def weigh(slot, index, valid_rows):
        group = min(tokens, LANES)
        for col in range(0, tokens, group):
            cols = slice(col, col + group)
            target = labels_ref[:, cols] - index * tile
            own, other, gap = (pick_row(ref[:, cols], index) for ref in (a_ref, b_ref, g_ref))
            cross = c_ref[:, cols]
            for start, rows, valid in chunks(valid_rows):
                here = slice(start, start + rows)
                row = lax.broadcasted_iota(jnp.int32, (rows, group), 0)
                student = ps_ref[here, cols].astype(jnp.float32) * own
                teacher = pt_ref[here, cols].astype(jnp.float32) * other
                lowered = l_ref[here, cols].astype(jnp.float32)
                part = teacher * (gap - lowered)
                value = student - teacher - jnp.where(row == target - start, scale, 0.0)
                if valid < rows:
                    part = jnp.where(row < valid, part, 0.0)
                    value = jnp.where(row < valid, value, 0.0)
                cross = cross + jnp.sum(part, axis=0, keepdims=True)
                value = value.astype(jnp.bfloat16)
                d_ref[here, cols] = value
                d_scratch[slot, here, cols] = value
            c_ref[:, cols] = cross

    def matmul(slot, valid_rows):
        depth = cdiv(valid_rows, 16) * 16
        if valid_rows % 16:
            edge = slice(depth - 16, depth)
            row = lax.broadcasted_iota(jnp.int32, (16, w_ref.shape[1]), 0)
            w_ref[edge, :] = jnp.where(row < valid_rows - depth + 16, w_ref[edge, :], jnp.zeros((), w_ref.dtype))
        for start in range(0, up_ref.shape[1], 512):
            out = slice(start, start + 512)
            up_ref[:, out] += lax.dot_general(
                d_scratch[slot, :depth, :], w_ref[:depth, out], (((0,), (0,)), ((), ())),
                preferred_element_type=jnp.float32,
            )

    @pl.when(step == 0)
    def _():
        own_total, other_total = totals_ref[0:1, :], totals_ref[1:2, :]
        a_ref[...] = jnp.exp(ms_ref[...] - own_total) * ((1.0 + BETA) * scale)
        b_ref[...] = jnp.exp(mt_ref[...] - other_total) * (BETA * scale)
        g_ref[...] = own_total - ms_ref[...]
        c_ref[...] = jnp.zeros_like(c_ref)
        up_ref[...] = jnp.zeros_like(up_ref)
        weigh(0, 0, last_rows if tiles == 1 else tile)

    if tiles > 2:

        @pl.when((step > 0) & (step < tiles - 1))
        def _():
            matmul(lax.rem(step + 1, 2), tile)
            weigh(lax.rem(step, 2), step, tile)

    if tiles > 1:

        @pl.when(step == tiles - 1)
        def _():
            matmul(tiles % 2, tile)
            weigh((tiles - 1) % 2, tiles - 1, last_rows)

    @pl.when(step == tiles)
    def _():
        matmul((tiles - 1) % 2, last_rows)
        cross_ref[...] = jnp.broadcast_to(c_ref[...] * (tokens / BETA), cross_ref.shape)


def run_dlogits(totals, labels, m_own, m_other, p_own, p_other, lowered, weights):
    tokens = p_own.shape[1]
    vocab_dev, width = weights.shape
    tile, tiles = tiling(vocab_dev)
    groups = m_own.shape[0]
    here = pl.BlockSpec((tile, tokens), lambda j: (jnp.minimum(j, tiles - 1), 0))
    return pl.pallas_call(
        functools.partial(dlogits_kernel, vocab_dev, tile, tiles),
        grid=(tiles + 1,),
        in_specs=[
            whole((8, tokens)),
            whole((1, tokens)),
            whole((groups, tokens)),
            whole((groups, tokens)),
            here,
            here,
            here,
            pl.BlockSpec((tile, width), lambda j: (jnp.maximum(j - 1, 0), 0)),
        ],
        out_specs=[here, whole((tokens, width)), whole((8, tokens))],
        out_shape=[
            jax.ShapeDtypeStruct((vocab_dev, tokens), jnp.bfloat16),
            jax.ShapeDtypeStruct((tokens, width), jnp.float32),
            jax.ShapeDtypeStruct((8, tokens), jnp.float32),
        ],
        scratch_shapes=[
            pltpu.VMEM((2, tile, tokens), jnp.bfloat16),
            pltpu.VMEM((groups, tokens), jnp.float32),
            pltpu.VMEM((groups, tokens), jnp.float32),
            pltpu.VMEM((groups, tokens), jnp.float32),
            pltpu.VMEM((1, tokens), jnp.float32),
        ],
        compiler_params=pltpu.CompilerParams(vmem_limit_bytes=VMEM_LIMIT),
        cost_estimate=pl.CostEstimate(
            flops=2 * tokens * width * vocab_dev,
            bytes_accessed=2 * width * vocab_dev + 8 * tokens * vocab_dev,
            transcendentals=0,
        ),
        name="dlogits",
    )(totals, labels, m_own, m_other, p_own, p_other, lowered, weights)


def head_grad_kernel(normed_ref, d_ref, out_ref):
    out_ref[...] = jnp.dot(d_ref[...], normed_ref[...], preferred_element_type=jnp.float32).astype(out_ref.dtype)


def run_head_grad(normed, dlogits):
    tokens, width = normed.shape
    vocab_dev = dlogits.shape[0]
    tile, tiles = tiling(vocab_dev)
    return pl.pallas_call(
        head_grad_kernel,
        grid=(tiles,),
        in_specs=[whole((tokens, width)), pl.BlockSpec((tile, tokens), lambda j: (j, 0))],
        out_specs=pl.BlockSpec((tile, width), lambda j: (j, 0)),
        out_shape=jax.ShapeDtypeStruct((vocab_dev, width), jnp.bfloat16),
        compiler_params=pltpu.CompilerParams(vmem_limit_bytes=VMEM_LIMIT),
        cost_estimate=pl.CostEstimate(
            flops=2 * tokens * width * vocab_dev,
            bytes_accessed=2 * width * vocab_dev + 2 * tokens * vocab_dev,
            transcendentals=0,
        ),
        name="head_grad",
    )(normed, dlogits)


def gather_blocks(own, bits):
    held = own[None]
    for bit in reversed(range(bits)):
        arrived = flip_bit(held, "fsdp", bit)
        held = jnp.stack([held, arrived])
        held = held.reshape((-1,) + own.shape)
    return held


def place_bits(bits):
    offsets = [0]
    for bit in reversed(range(bits)):
        offsets = offsets + [o | 1 << bit for o in offsets]
    return offsets


def swap_halves(value, axis):
    low, high = jnp.split(value, 2, axis=axis)
    return jnp.concatenate([high, low], axis=axis)


def merge(own, other):
    top = jnp.maximum(own[0::3], other[0::3])
    total = own[1::3] * jnp.exp(own[0::3] - top) + other[1::3] * jnp.exp(other[0::3] - top)
    picked = own[2::3] + other[2::3]
    parts = []
    for i in range(top.shape[0]):
        parts += [top[i : i + 1], total[i : i + 1], picked[i : i + 1]]
    return jnp.concatenate(parts, axis=0)


def body(hidden, gain, head, labels):
    own_rows = hidden[0]
    gain_row = gain[0]
    weights = head[0].T
    tok_dev, width = own_rows.shape
    vocab_dev = weights.shape[0]
    count = lax.axis_size("fsdp")
    bits = count.bit_length() - 1
    index = lax.axis_index("fsdp")
    tokens = tok_dev * count

    rows = gather_blocks(own_rows, bits).reshape(tokens, width)
    offsets = jnp.asarray(place_bits(bits), jnp.int32)
    local_labels = (
        labels.reshape(count, tok_dev)[offsets ^ index].reshape(1, tokens) - index * vocab_dev
    )

    p_own, lowered, normed, m_own, stats = run_logits(rows, gain_row[None], local_labels, weights)

    p_other = flip_bit(p_own, "member", 0)
    m_other = flip_bit(m_own, "member", 0)

    table = stats[:3]
    for bit in range(bits):
        arrived = flip_bit(table, "fsdp", bit)
        place = bits - 1 - bit
        block = tok_dev << place
        arrived = swap_halves(arrived.reshape(3, tokens // (2 * block), 2 * block), 2).reshape(3, tokens)
        table = merge(table, arrived)
    log_total = table[0] + jnp.log(table[1])
    picked = table[2]
    other_total = flip_bit(log_total, "member", 0)
    totals = jnp.concatenate([log_total[None], other_total[None], jnp.zeros((6, tokens), jnp.float32)])

    dlogits, partial_up, cross = run_dlogits(
        totals, local_labels, m_own, m_other, p_own, p_other, lowered, weights
    )

    summed = partial_up
    cross_sum = cross[0]
    for bit in range(bits):
        half = summed.shape[0] // 2
        arrived = flip_bit(summed[half:].astype(jnp.bfloat16), "fsdp", bit)
        summed = summed[:half] + arrived.astype(jnp.float32)
        arrived = flip_bit(cross_sum[half:], "fsdp", bit)
        cross_sum = cross_sum[:half] + arrived

    head_grad = run_head_grad(normed, dlogits).T

    token_loss = log_total[:tok_dev] - picked[:tok_dev] + BETA * cross_sum
    values = own_rows.astype(jnp.float32)
    inverse = lax.rsqrt(jnp.mean(values * values, axis=-1, keepdims=True) + EPS)
    scaled = gain_row * summed
    inner = jnp.mean(scaled * values, axis=-1, keepdims=True)
    hidden_grad = inverse * scaled - values * inverse**3 * inner
    return (token_loss[None], head_grad[None], hidden_grad.astype(jnp.bfloat16)[None])


def solution(mesh):
    in_specs = (P("member", "fsdp", None), P("member", None), P("member", None, "fsdp"), P())
    out_specs = (P("member", "fsdp"), P("member", None, "fsdp"), P("member", "fsdp", None))
    return jax.shard_map(body, mesh=mesh, in_specs=in_specs, out_specs=out_specs, check_vma=False)
```

```python
import functools
import jax
import jax.numpy as jnp
from jax import lax
from jax.experimental import pallas as pl
from jax.experimental.pallas import tpu as pltpu
from jax.sharding import PartitionSpec as P

EPS = 1e-05
BETA = 0.5
TILE = 1024
CHUNK = 128
LANES = 128
VMEM_SHARED = 24 * 1024 * 1024
VMEM_ALONE = 40 * 1024 * 1024
GRAD_EDGES = (0, 3, 5, 8)
LOAD_COPIES = 4
SMALL = pl.CostEstimate(flops=4096, bytes_accessed=4096, transcendentals=0)


def cdiv(a, b):
    return -(-a // b)


def tiling(vocab_dev):
    tile = min(TILE, vocab_dev)
    return tile, cdiv(vocab_dev, tile)


def whole(shape):
    return pl.BlockSpec(shape, lambda j: (0, 0))


def whole_vmem():
    return pl.BlockSpec(memory_space=pltpu.VMEM)


def pinned(value):
    return pltpu.with_memory_space_constraint(value, pltpu.VMEM)


def chunks(valid):
    return [(start, min(CHUNK, valid - start)) for start in range(0, valid, CHUNK)]


def pick_row(table, index):
    here = lax.broadcasted_iota(jnp.int32, table.shape, 0) == index
    return jnp.sum(jnp.where(here, table, 0.0), axis=0, keepdims=True)


def load_kernel(first, rows, w_ref, *refs):
    out_ref, sems = refs[-2:]
    pieces = []
    step = cdiv(cdiv(rows, LOAD_COPIES), 16) * 16
    for i, start in enumerate(range(0, rows, step)):
        piece = pl.ds(first + start, min(step, rows - start))
        pieces.append(pltpu.make_async_copy(w_ref.at[piece, :], out_ref.at[piece, :], sems.at[i]))
    for piece in pieces:
        piece.start()
    for piece in pieces:
        piece.wait()


def run_load(first, rows, weights, after, held):
    operands, in_specs, aliases = [weights, after], [pl.BlockSpec(memory_space=pl.ANY)] * 2, {}
    if held is not None:
        operands.append(held)
        in_specs.append(whole_vmem())
        aliases[2] = 0
    return pl.pallas_call(
        functools.partial(load_kernel, first, rows),
        in_specs=in_specs,
        out_specs=whole_vmem(),
        out_shape=pltpu.VMEM(weights.shape, weights.dtype),
        scratch_shapes=[pltpu.SemaphoreType.DMA((LOAD_COPIES,))],
        input_output_aliases=aliases,
        compiler_params=pltpu.CompilerParams(vmem_limit_bytes=VMEM_SHARED),
        cost_estimate=pl.CostEstimate(flops=0, bytes_accessed=4 * rows * weights.shape[1], transcendentals=0),
        name="load",
    )(*operands)


def join_kernel(count, split, *refs):
    pieces, outs = refs[:count], refs[-2 if split else -1 :]
    for i, piece in enumerate(pieces):
        half = piece.shape[0] // 2
        for part in range(2):
            rows = piece[part * half : (part + 1) * half, :]
            if split:
                outs[part][i * half : (i + 1) * half, :] = rows
            else:
                place = (part * count + i) * half
                outs[0][place : place + half, :] = rows


def run_join(pieces, split, weights):
    rows, width = pieces[0].shape
    total = rows * len(pieces)
    kind = lambda n: jax.ShapeDtypeStruct((n, width), pieces[0].dtype)
    return pl.pallas_call(
        functools.partial(join_kernel, len(pieces), split),
        in_specs=[whole_vmem()] * (len(pieces) + 1),
        out_specs=[whole_vmem()] * (2 if split else 1),
        out_shape=[kind(total // 2)] * 2 if split else [kind(total)],
        compiler_params=pltpu.CompilerParams(vmem_limit_bytes=VMEM_SHARED),
        cost_estimate=SMALL,
        name="join",
    )(*pieces, weights)


def stack_kernel(w_ref, low_a, high_a, low_b, high_b, a_ref, b_ref):
    half = low_a.shape[0]
    for low, high, out in ((low_a, high_a, a_ref), (low_b, high_b, b_ref)):
        out[:half, :] = low[...]
        out[half:, :] = high[...]


def run_stack(weights, *pieces):
    rows, width = pieces[0].shape
    return pl.pallas_call(
        stack_kernel,
        in_specs=[whole_vmem()] * 5,
        out_specs=[whole_vmem()] * 2,
        out_shape=[jax.ShapeDtypeStruct((2 * rows, width), pieces[0].dtype)] * 2,
        cost_estimate=SMALL,
        compiler_params=pltpu.CompilerParams(vmem_limit_bytes=VMEM_SHARED),
        name="stack",
    )(weights, *pieces)


def merge_kernel(count, lanes, final, table_ref, *refs):
    arrived, out_ref = refs[:count], refs[-1]
    tokens = table_ref.shape[1]
    lane = lax.broadcasted_iota(jnp.int32, (8, tokens), 1)

    def swap(value, stride):
        return jnp.where(
            lane & stride == 0, pltpu.roll(value, tokens - stride, 1), pltpu.roll(value, stride, 1)
        )

    tables = [table_ref[...]]
    for ref, moves in zip(arrived, lanes):
        value = ref[...]
        for stride_a, stride_b, part in moves:
            if stride_a == stride_b:
                value = swap(value, stride_a)
            else:
                value = jnp.where(lane & part == 0, swap(value, stride_a), swap(value, stride_b))
        tables.append(value)
    top = functools.reduce(jnp.maximum, [t[0:1] for t in tables])
    total = sum(t[1:2] * jnp.exp(t[0:1] - top) for t in tables)
    picked = sum(t[2:3] for t in tables)
    out_ref[0:8, :] = jnp.zeros((8, tokens), jnp.float32)
    if final:
        out_ref[0:1, :] = top + jnp.log(total)
        out_ref[1:2, :] = picked
        out_ref[8:, :] = refs[count][...]
    else:
        out_ref[0:1, :] = top
        out_ref[1:2, :] = total
        out_ref[2:3, :] = picked


def run_merge(weights, table, arrived, lanes, tops):
    operands = [table, *arrived] + ([] if tops is None else [tops]) + [weights]
    rows = 8 + (0 if tops is None else tops.shape[0])
    return pl.pallas_call(
        functools.partial(merge_kernel, len(arrived), lanes, tops is not None),
        in_specs=[whole_vmem()] * len(operands),
        out_specs=whole_vmem(),
        out_shape=jax.ShapeDtypeStruct((rows, table.shape[1]), jnp.float32),
        compiler_params=pltpu.CompilerParams(vmem_limit_bytes=VMEM_SHARED),
        cost_estimate=SMALL,
        name="totals",
    )(*operands)


def logits_kernel(
    tile, tiles, group_index, rows_a_ref, rows_b_ref, gain_ref, labels_ref, w_ref, *refs
):
    p_ref, l_ref, normed_ref, tops_ref, stats_ref, logits_ref, m_ref, s_ref, picked_ref = refs[-9:]
    step = pl.program_id(0)
    tokens = normed_ref.shape[0]
    last_rows = w_ref.shape[0] - (tiles - 1) * tile

    def matmul(slot, start, rows):
        logits_ref[slot, :rows, :] = lax.dot_general(
            w_ref[pl.ds(start, rows), :], normed_ref[...], (((1,), (1,)), ((), ())),
            preferred_element_type=jnp.float32,
        )

    def soften(slot, index, valid_rows):
        group = min(tokens, LANES)
        for col in range(0, tokens, group):
            cols = slice(col, col + group)
            target = labels_ref[:, group_index * tokens + col : group_index * tokens + col + group] - index * tile
            top = None
            for start, rows in chunks(valid_rows):
                part = jnp.max(logits_ref[slot, start : start + rows, cols], axis=0, keepdims=True)
                top = part if top is None else jnp.maximum(top, part)
            total = jnp.zeros((1, group), jnp.float32)
            picked = picked_ref[:, cols]
            for start, rows in chunks(valid_rows):
                values = logits_ref[slot, start : start + rows, cols]
                row = lax.broadcasted_iota(jnp.int32, (rows, group), 0)
                lowered = values - top
                exps = jnp.exp(lowered)
                l_ref[start : start + rows, cols] = lowered.astype(l_ref.dtype)
                p_ref[start : start + rows, cols] = exps.astype(p_ref.dtype)
                chosen = jnp.where(row == target - start, values, 0.0)
                total = total + jnp.sum(exps, axis=0, keepdims=True)
                picked = picked + jnp.sum(chosen, axis=0, keepdims=True)
            here = lax.broadcasted_iota(jnp.int32, (m_ref.shape[0], group), 0) == index
            m_ref[:, cols] = jnp.where(here, top, m_ref[:, cols])
            s_ref[:, cols] = jnp.where(here, total, s_ref[:, cols])
            picked_ref[:, cols] = picked

    @pl.when(step == 0)
    def _():
        half = tokens // 2
        for place, rows_ref in ((0, rows_a_ref), (half, rows_b_ref)):
            values = rows_ref[...].astype(jnp.float32)
            inverse = lax.rsqrt(jnp.mean(values * values, axis=-1, keepdims=True) + EPS)
            normed_ref[place : place + half, :] = (values * inverse * gain_ref[...]).astype(jnp.bfloat16)
        m_ref[...] = jnp.full_like(m_ref, -jnp.inf)
        s_ref[...] = jnp.zeros_like(s_ref)
        picked_ref[...] = jnp.zeros_like(picked_ref)
        matmul(0, 0, last_rows if tiles == 1 else tile)

    if tiles > 2:

        @pl.when((step > 0) & (step < tiles - 1))
        def _():
            matmul(lax.rem(step, 2), pl.multiple_of(step * tile, tile), tile)
            soften(lax.rem(step + 1, 2), step - 1, tile)

    if tiles > 1:

        @pl.when(step == tiles - 1)
        def _():
            matmul((tiles - 1) % 2, (tiles - 1) * tile, last_rows)
            soften(tiles % 2, tiles - 2, tile)

    @pl.when(step == tiles)
    def _():
        soften((tiles - 1) % 2, tiles - 1, last_rows)
        tops = m_ref[...]
        top = jnp.max(tops, axis=0, keepdims=True)
        total = jnp.sum(s_ref[...] * jnp.exp(tops - top), axis=0, keepdims=True)
        place = group_index * tokens
        cols = slice(place, place + tokens)
        if group_index:
            stats_ref[:, :place] = refs[1][...]
            tops_ref[:, :place] = refs[2][...]
        tops_ref[:, cols] = tops
        stats_ref[:, cols] = jnp.zeros((8, tokens), jnp.float32)
        stats_ref[0:1, cols] = top
        stats_ref[1:2, cols] = total
        stats_ref[2:3, cols] = picked_ref[...]


def run_logits(group, rows_a, rows_b, gain, labels, weights, before):
    half, width = rows_a.shape
    tokens = 2 * half
    vocab_dev = weights.shape[0]
    tile, tiles = tiling(vocab_dev)
    groups = cdiv(tiles, 8) * 8
    behind = pl.BlockSpec((tile, tokens), lambda j: (jnp.maximum(j - 1, 0), 0))
    operands = [rows_a, rows_b, gain, labels, weights]
    in_specs = [
        whole_vmem(),
        whole_vmem(),
        whole((1, width)),
        whole_vmem(),
        whole_vmem(),
    ]
    aliases = {}
    if group:
        aliases[len(operands)] = 2
        operands += before
        in_specs += [pl.BlockSpec(memory_space=pl.ANY), whole_vmem(), whole_vmem()]
    return pl.pallas_call(
        functools.partial(logits_kernel, tile, tiles, group),
        grid=(tiles + 1,),
        in_specs=in_specs,
        out_specs=[
            behind,
            behind,
            pl.BlockSpec((tokens, width), lambda j: (group, 0)),
            whole_vmem(),
            whole_vmem(),
        ],
        out_shape=[
            jax.ShapeDtypeStruct((vocab_dev, tokens), jnp.bfloat16),
            jax.ShapeDtypeStruct((vocab_dev, tokens), jnp.bfloat16),
            jax.ShapeDtypeStruct((2 * tokens, width), jnp.bfloat16),
            jax.ShapeDtypeStruct((groups, (group + 1) * tokens), jnp.float32),
            jax.ShapeDtypeStruct((8, (group + 1) * tokens), jnp.float32),
        ],
        scratch_shapes=[
            pltpu.VMEM((2, tile, tokens), jnp.float32),
            pltpu.VMEM((groups, tokens), jnp.float32),
            pltpu.VMEM((groups, tokens), jnp.float32),
            pltpu.VMEM((1, tokens), jnp.float32),
        ],
        input_output_aliases=aliases,
        compiler_params=pltpu.CompilerParams(vmem_limit_bytes=VMEM_SHARED),
        cost_estimate=pl.CostEstimate(
            flops=2 * tokens * width * vocab_dev,
            bytes_accessed=4 * tokens * vocab_dev,
            transcendentals=tokens * vocab_dev,
        ),
        name="logits",
    )(*operands)


def dlogits_kernel(
    tile, tiles, group_index, own_ref, other_ref, labels_ref, ps_ref, pt_ref, l_ref, w_ref, *refs
):
    d_ref, first_ref, second_ref, up_ref, d_scratch, a_ref, b_ref, g_ref, c_ref = refs[-9:]
    step = pl.program_id(0)
    tokens = ps_ref.shape[1]
    all_tokens = labels_ref.shape[1]
    first = group_index * tokens
    scale = 1.0 / all_tokens
    last_rows = w_ref.shape[0] - (tiles - 1) * tile

    def weigh(slot, index, valid_rows):
        group = min(tokens, LANES)
        for col in range(0, tokens, group):
            cols = slice(col, col + group)
            target = labels_ref[:, first + col : first + col + group] - index * tile
            own, other, gap = (pick_row(ref[:, cols], index) for ref in (a_ref, b_ref, g_ref))
            cross = c_ref[:, cols]
            for start, rows in chunks(valid_rows):
                here = slice(start, start + rows)
                row = lax.broadcasted_iota(jnp.int32, (rows, group), 0)
                student = ps_ref[here, cols].astype(jnp.float32) * own
                teacher = pt_ref[here, cols].astype(jnp.float32) * other
                lowered = l_ref[here, cols].astype(jnp.float32)
                part = teacher * (gap - lowered)
                value = student - teacher - jnp.where(row == target - start, scale, 0.0)
                cross = cross + jnp.sum(part, axis=0, keepdims=True)
                value = value.astype(jnp.bfloat16)
                d_ref[here, cols] = value
                d_scratch[slot, here, cols] = value
            c_ref[:, cols] = cross

    def matmul(slot, start, rows):
        for out in range(0, up_ref.shape[1], 512):
            cols = slice(out, out + 512)
            up_ref[:, cols] += lax.dot_general(
                d_scratch[slot, :rows, :], w_ref[pl.ds(start, rows), cols], (((0,), (0,)), ((), ())),
                preferred_element_type=jnp.float32,
            )

    @pl.when(step == 0)
    def _():
        here = slice(first, first + tokens)
        own_total, other_total = own_ref[0:1, here], other_ref[0:1, here]
        a_ref[...] = jnp.exp(own_ref[8:, here] - own_total) * ((1.0 + BETA) * scale)
        b_ref[...] = jnp.exp(other_ref[8:, here] - other_total) * (BETA * scale)
        g_ref[...] = own_total - own_ref[8:, here]
        c_ref[...] = jnp.zeros_like(c_ref)
        up_ref[...] = jnp.zeros_like(up_ref)
        weigh(0, 0, last_rows if tiles == 1 else tile)

    if tiles > 2:

        @pl.when((step > 0) & (step < tiles - 1))
        def _():
            matmul(lax.rem(step + 1, 2), pl.multiple_of((step - 1) * tile, tile), tile)
            weigh(lax.rem(step, 2), step, tile)

    if tiles > 1:

        @pl.when(step == tiles - 1)
        def _():
            matmul(tiles % 2, (tiles - 2) * tile, tile)
            weigh((tiles - 1) % 2, tiles - 1, last_rows)

    @pl.when(step == tiles)
    def _():
        matmul((tiles - 1) % 2, (tiles - 1) * tile, last_rows)
        width = up_ref.shape[1]
        half = tokens // 2
        column = jnp.broadcast_to(c_ref[...] * (all_tokens / BETA), (LANES, tokens)).T
        lane = lax.broadcasted_iota(jnp.int32, (tokens, LANES), 1)
        if first_ref.dtype == jnp.float32:
            edge = jnp.where(lane == 0, column, 0.0)
        else:
            high = column.astype(jnp.bfloat16).astype(jnp.float32)
            edge = jnp.where(lane == 0, high, jnp.where(lane == 1, column - high, 0.0))
        for ref, place in ((first_ref, 0), (second_ref, half)):
            ref[:, :width] = up_ref[place : place + half, :].astype(ref.dtype)
            ref[:, width:] = edge[place : place + half, :].astype(ref.dtype)


def run_dlogits(group, totals, other_totals, labels, p_own, p_other, lowered, weights, dlogits, out_type):
    tokens = p_own.shape[1]
    vocab_dev, width = weights.shape
    tile, tiles = tiling(vocab_dev)
    groups = totals.shape[0] - 8
    wide = width + LANES
    ahead = lambda j: jnp.minimum(j, tiles - 1)
    here = pl.BlockSpec((tile, tokens), lambda j: (ahead(j), 0))
    p_own, p_other, lowered = (pltpu.with_memory_space_constraint(v, pltpu.HBM) for v in (p_own, p_other, lowered))
    operands = [totals, other_totals, labels, p_own, p_other, lowered, weights]
    in_specs = [
        whole_vmem(),
        whole_vmem(),
        whole_vmem(),
        here,
        here,
        here,
        pl.BlockSpec(memory_space=pltpu.VMEM),
    ]
    aliases = {}
    if dlogits is not None:
        aliases[len(operands)] = 0
        operands.append(dlogits)
        in_specs.append(pl.BlockSpec(memory_space=pl.ANY))
    return pl.pallas_call(
        functools.partial(dlogits_kernel, tile, tiles, group),
        grid=(tiles + 1,),
        in_specs=in_specs,
        out_specs=[
            pl.BlockSpec((tile, tokens), lambda j: (ahead(j), group)),
            whole_vmem(),
            whole_vmem(),
        ],
        out_shape=[
            jax.ShapeDtypeStruct((vocab_dev, 2 * tokens), jnp.bfloat16),
            jax.ShapeDtypeStruct((tokens // 2, wide), out_type),
            jax.ShapeDtypeStruct((tokens // 2, wide), out_type),
        ],
        scratch_shapes=[
            pltpu.VMEM((tokens, width), jnp.float32),
            pltpu.VMEM((2, tile, tokens), jnp.bfloat16),
            pltpu.VMEM((groups, tokens), jnp.float32),
            pltpu.VMEM((groups, tokens), jnp.float32),
            pltpu.VMEM((groups, tokens), jnp.float32),
            pltpu.VMEM((1, tokens), jnp.float32),
        ],
        input_output_aliases=aliases,
        compiler_params=pltpu.CompilerParams(vmem_limit_bytes=VMEM_SHARED),
        cost_estimate=pl.CostEstimate(
            flops=2 * tokens * width * vocab_dev,
            bytes_accessed=8 * tokens * vocab_dev,
            transcendentals=0,
        ),
        name="dlogits",
    )(*operands)


def fold_kernel(count, gots, sends, *refs):
    sums, arrived, outs = refs[:count], refs[count : count + gots], refs[-1 - sends :]
    keep, send = outs[0], outs[1:]
    width = keep.shape[2] - LANES
    cut = keep.shape[1]
    lane = lax.broadcasted_iota(jnp.int32, (cut, LANES), 1)
    for part in range(2):
        held = sums[part][...] if count == 2 else sums[0][part]
        got = arrived[part][...] if gots == 2 else arrived[0][part]
        total = held + got.astype(jnp.float32)
        keep[part] = total[:cut]
        gone = total[cut:]
        cross = gone[:, width : width + 1] + gone[:, width + 1 : width + 2]
        high = cross.astype(jnp.bfloat16).astype(jnp.float32)
        edge = jnp.where(lane == 0, high, jnp.where(lane == 1, cross - high, 0.0))
        value = jnp.concatenate([gone[:, :width], edge], axis=1).astype(jnp.bfloat16)
        if sends == 2:
            send[part][...] = value
        else:
            send[0][part] = value


def run_fold(sums, arrived, sends, after):
    rows, wide = sums[0].shape[-2:]
    cut = rows // 2
    operands = list(sums) + list(arrived)
    in_specs = [pl.BlockSpec(memory_space=pltpu.VMEM)] * len(operands)
    if after is not None:
        operands.append(pltpu.with_memory_space_constraint(after, pltpu.HBM))
        in_specs.append(pl.BlockSpec(memory_space=pl.ANY))
    shape = (cut, wide) if sends == 2 else (2, cut, wide)
    return pl.pallas_call(
        functools.partial(fold_kernel, len(sums), len(arrived), sends),
        in_specs=in_specs,
        out_specs=[pl.BlockSpec(memory_space=pltpu.VMEM)] * (1 + sends),
        out_shape=[jax.ShapeDtypeStruct((2, cut, wide), jnp.float32)]
        + [jax.ShapeDtypeStruct(shape, jnp.bfloat16)] * sends,
        compiler_params=pltpu.CompilerParams(vmem_limit_bytes=VMEM_SHARED),
        cost_estimate=SMALL,
        name="fold",
    )(*operands)


def head_grad_kernel(normed_ref, d_ref, *refs):
    out_ref = refs[-1]
    out_ref[...] = jnp.dot(d_ref[...], normed_ref[...], preferred_element_type=jnp.float32).astype(out_ref.dtype)


def run_head_grad(first, count, normed, dlogits, grad, after):
    tokens, width = normed.shape
    vocab_dev = dlogits.shape[0]
    tile, tiles = tiling(vocab_dev)
    operands = [normed, pltpu.with_memory_space_constraint(dlogits, pltpu.HBM)]
    in_specs = [whole((tokens, width)), pl.BlockSpec((tile, tokens), lambda j: (first + j, 0))]
    aliases = {}
    for value in after:
        operands.append(value)
        in_specs.append(pl.BlockSpec(memory_space=pl.ANY))
    if grad is not None:
        aliases[len(operands)] = 0
        operands.append(pltpu.with_memory_space_constraint(grad, pltpu.HBM))
        in_specs.append(pl.BlockSpec(memory_space=pl.ANY))
    return pl.pallas_call(
        head_grad_kernel,
        grid=(count,),
        in_specs=in_specs,
        out_specs=pl.BlockSpec((tile, width), lambda j: (first + j, 0)),
        out_shape=jax.ShapeDtypeStruct((vocab_dev, width), jnp.bfloat16),
        input_output_aliases=aliases,
        compiler_params=pltpu.CompilerParams(vmem_limit_bytes=VMEM_ALONE),
        cost_estimate=pl.CostEstimate(
            flops=2 * tokens * width * tile * count,
            bytes_accessed=2 * width * tile * count + 2 * tokens * tile * count,
            transcendentals=0,
        ),
        name="head_grad",
    )(*operands)


def moved(value, offset):
    n = lax.axis_size("fsdp")
    return lax.ppermute(value, "fsdp", [(i, i ^ offset) for i in range(n)])


def other_member(value):
    return lax.ppermute(value, "member", [(0, 1), (1, 0)])


def token_order(bits):
    offsets = [0]
    for bit in reversed(range(2, bits)):
        offsets = offsets + [o | 1 << bit for o in offsets]
    order = []
    for group in range(2):
        for half in range(2):
            group_bit, place_bit = (1, 2) if half == 0 else (2, 1)
            for place in range(2):
                order += [(group * group_bit + place * place_bit + o, half) for o in offsets]
    return order


def lane_moves(offset, bits, half):
    moves = []
    for bit in range(bits):
        if offset >> bit & 1:
            group, place = half << bits, half << (bits - 2)
            strides = {0: (group, place), 1: (place, group)}.get(bit, (half << (bits - 1 - bit),) * 2)
            moves.append(strides + (half << (bits - 1),))
    return tuple(moves)


def pack(value, width):
    cross = value[..., width : width + 1] + value[..., width + 1 : width + 2]
    high = lax.reduce_precision(cross, 8, 7)
    rest = jnp.zeros(value.shape[:-1] + (LANES - 2,), jnp.float32)
    return jnp.concatenate([value[..., :width], high, cross - high, rest], axis=-1).astype(jnp.bfloat16)


def body(hidden, gain, head, labels):
    own_rows = hidden[0]
    gain_row = gain[0]
    tok_dev, width = own_rows.shape
    vocab_dev = head.shape[2]
    count = lax.axis_size("fsdp")
    bits = count.bit_length() - 1
    index = lax.axis_index("fsdp")
    half = tok_dev // 2
    tokens = tok_dev * count

    order = token_order(bits)
    offsets = jnp.asarray([o for o, _ in order], jnp.int32)
    halves = jnp.asarray([s for _, s in order], jnp.int32)
    local_labels = labels.reshape(2 * count, half)[(offsets ^ index) * 2 + halves].reshape(1, tokens)
    local_labels = local_labels - index * vocab_dev

    first_rows = min(vocab_dev, cdiv(vocab_dev // 2, 16) * 16)
    weights = pinned(run_load(0, first_rows, head[0].T, local_labels, None))
    held = [own_rows]
    for bit in reversed(range(2, bits)):
        held = run_join([held[0], moved(held[0], 1 << bit)], bit == 2, weights)
        if bit == bits - 1 and first_rows < vocab_dev:
            weights = pinned(run_load(first_rows, vocab_dev - first_rows, head[0].T, held[0], weights))
    near_a, near_b = run_stack(weights, held[0], moved(held[0], 2), held[1], moved(held[1], 1))
    far_a = moved(near_a, 1)
    far_b = moved(near_b, 2)

    p_near, l_near, normed, tops, stats = run_logits(
        0, near_a, near_b, gain_row[None], local_labels, weights, []
    )
    p_near_other = other_member(p_near)
    p_far, l_far, normed, tops, table = run_logits(
        1, far_a, far_b, gain_row[None], local_labels, weights, [normed, stats, tops]
    )
    p_far_other = other_member(p_far)

    for bit in range(0, bits, 2):
        steps = [k << bit for k in range(1, 4) if k << bit < count]
        lanes = [lane_moves(k, bits, half) for k in steps]
        table = run_merge(weights, table, [moved(table, k) for k in steps], lanes, tops if bit + 2 >= bits else None)
    other_totals = other_member(table)

    dlogits, send_a, send_b = run_dlogits(
        1, table, other_totals, local_labels, p_far, p_far_other, l_far, weights, None, jnp.bfloat16
    )
    got_a, got_b = moved(send_a, 1), moved(send_b, 2)
    dlogits, sum_a, sum_b = run_dlogits(
        0, table, other_totals, local_labels, p_near, p_near_other, l_near, weights, dlogits, jnp.float32
    )

    tile, tiles = tiling(vocab_dev)
    edges = [tiles * i // 8 for i in GRAD_EDGES]
    grad = None
    summed, sends = run_fold((sum_a, sum_b), (got_a, got_b), 2, None), 2
    for step in range(1, bits):
        keep, send = summed[0], summed[1:]
        if step <= 3 and edges[step] > edges[step - 1]:
            grad = run_head_grad(edges[step - 1], edges[step] - edges[step - 1], normed, dlogits, grad, send)
        if step == 1:
            got = [moved(send[0], 2), moved(send[1], 1)]
        else:
            got = [moved(send[0], 1 << step)]
        cut = keep.shape[1] // 2
        if step < bits - 1 and cut % 16 == 0:
            summed = run_fold((keep,), got, 1, grad)
        else:
            total = keep + (jnp.stack(got) if step == 1 else got[0]).astype(jnp.float32)
            if step < bits - 1:
                summed = [total[:, :cut], pack(total[:, cut:], width)]
            else:
                summed = total
    summed = summed.reshape(tok_dev, -1)
    cross = summed[:, width] + summed[:, width + 1]
    summed = summed[:, :width]

    quarter = tokens // 4
    own = lambda row: jnp.concatenate([row[:half], row[quarter : quarter + half]])
    token_loss = own(table[0]) - own(table[1]) + BETA * cross
    values = own_rows.astype(jnp.float32)
    inverse = lax.rsqrt(jnp.mean(values * values, axis=-1, keepdims=True) + EPS)
    scaled = gain_row * summed
    inner = jnp.mean(scaled * values, axis=-1, keepdims=True)
    hidden_grad = inverse * scaled - values * inverse**3 * inner
    return (token_loss[None], grad.T[None], hidden_grad.astype(jnp.bfloat16)[None])


def solution(mesh):
    in_specs = (P("member", "fsdp", None), P("member", None), P("member", None, "fsdp"), P())
    out_specs = (P("member", "fsdp"), P("member", None, "fsdp"), P("member", "fsdp", None))
    return jax.shard_map(body, mesh=mesh, in_specs=in_specs, out_specs=out_specs, check_vma=False)
```

```python
import functools
import jax
import jax.numpy as jnp
from jax import lax
from jax.experimental import pallas as pl
from jax.experimental.pallas import tpu as pltpu
from jax.sharding import PartitionSpec as P

EPS = 1e-05
BETA = 0.5
TILE = 1024
GRAD_TILE = 1024
CHUNK = 128
PIECE = 512
LANES = 128
VMEM_SHARED = 34200000
VMEM_ALONE = 40 * 1024 * 1024
GRAD_EDGES = (0, 3, 5, 8)
LOAD_COPIES = 4
SMALL = pl.CostEstimate(flops=4096, bytes_accessed=4096, transcendentals=0)


def cdiv(a, b):
    return -(-a // b)


def tiling(vocab_dev, tile):
    tile = min(tile, vocab_dev)
    return tile, cdiv(vocab_dev, tile)


def whole(shape):
    return pl.BlockSpec(shape, lambda j: (0, 0))


def whole_vmem():
    return pl.BlockSpec(memory_space=pltpu.VMEM)


def together(first, second):
    done = 0
    for i, work in enumerate(first):
        work()
        upto = len(second) * (i + 1) // len(first)
        for other in second[done:upto]:
            other()
        done = upto
    if not first:
        for other in second:
            other()


def pinned(value):
    return pltpu.with_memory_space_constraint(value, pltpu.VMEM)


def chunks(valid):
    return [(start, min(CHUNK, valid - start)) for start in range(0, valid, CHUNK)]


def pick_row(table, index):
    here = lax.broadcasted_iota(jnp.int32, table.shape, 0) == index
    return jnp.sum(jnp.where(here, table, 0.0), axis=0, keepdims=True)


def load_kernel(first, rows, w_ref, *refs):
    out_ref, sems = refs[-2:]
    pieces = []
    step = cdiv(cdiv(rows, LOAD_COPIES), 16) * 16
    for i, start in enumerate(range(0, rows, step)):
        piece = pl.ds(first + start, min(step, rows - start))
        pieces.append(pltpu.make_async_copy(w_ref.at[piece, :], out_ref.at[piece, :], sems.at[i]))
    for piece in pieces:
        piece.start()
    for piece in pieces:
        piece.wait()


def run_load(first, rows, weights, after, held):
    operands, in_specs, aliases = [weights, after], [pl.BlockSpec(memory_space=pl.ANY)] * 2, {}
    if held is not None:
        operands.append(held)
        in_specs.append(whole_vmem())
        aliases[2] = 0
    return pl.pallas_call(
        functools.partial(load_kernel, first, rows),
        in_specs=in_specs,
        out_specs=whole_vmem(),
        out_shape=pltpu.VMEM(weights.shape, weights.dtype),
        scratch_shapes=[pltpu.SemaphoreType.DMA((LOAD_COPIES,))],
        input_output_aliases=aliases,
        compiler_params=pltpu.CompilerParams(vmem_limit_bytes=VMEM_SHARED),
        cost_estimate=pl.CostEstimate(flops=0, bytes_accessed=4 * rows * weights.shape[1], transcendentals=0),
        name="load",
    )(*operands)


def join_kernel(count, split, *refs):
    pieces, outs = refs[:count], refs[-2 if split else -1 :]
    for i, piece in enumerate(pieces):
        half = piece.shape[0] // 2
        for part in range(2):
            rows = piece[part * half : (part + 1) * half, :]
            if split:
                outs[part][i * half : (i + 1) * half, :] = rows
            else:
                place = (part * count + i) * half
                outs[0][place : place + half, :] = rows


def run_join(pieces, split, weights):
    rows, width = pieces[0].shape
    total = rows * len(pieces)
    kind = lambda n: jax.ShapeDtypeStruct((n, width), pieces[0].dtype)
    return pl.pallas_call(
        functools.partial(join_kernel, len(pieces), split),
        in_specs=[whole_vmem()] * (len(pieces) + 1),
        out_specs=[whole_vmem()] * (2 if split else 1),
        out_shape=[kind(total // 2)] * 2 if split else [kind(total)],
        compiler_params=pltpu.CompilerParams(vmem_limit_bytes=VMEM_SHARED),
        cost_estimate=SMALL,
        name="join",
    )(*pieces, weights)


def stack_kernel(w_ref, low_a, high_a, low_b, high_b, a_ref, b_ref):
    half = low_a.shape[0]
    for low, high, out in ((low_a, high_a, a_ref), (low_b, high_b, b_ref)):
        out[:half, :] = low[...]
        out[half:, :] = high[...]


def run_stack(weights, *pieces):
    rows, width = pieces[0].shape
    return pl.pallas_call(
        stack_kernel,
        in_specs=[whole_vmem()] * 5,
        out_specs=[whole_vmem()] * 2,
        out_shape=[jax.ShapeDtypeStruct((2 * rows, width), pieces[0].dtype)] * 2,
        cost_estimate=SMALL,
        compiler_params=pltpu.CompilerParams(vmem_limit_bytes=VMEM_SHARED),
        name="stack",
    )(weights, *pieces)


def merge_kernel(count, lanes, final, table_ref, *refs):
    arrived, out_ref = refs[:count], refs[-1]
    tokens = table_ref.shape[1]
    lane = lax.broadcasted_iota(jnp.int32, (8, tokens), 1)

    def swap(value, stride):
        return jnp.where(
            lane & stride == 0, pltpu.roll(value, tokens - stride, 1), pltpu.roll(value, stride, 1)
        )

    tables = [table_ref[...]]
    for ref, moves in zip(arrived, lanes):
        value = ref[...]
        for stride_a, stride_b, part in moves:
            if stride_a == stride_b:
                value = swap(value, stride_a)
            else:
                value = jnp.where(lane & part == 0, swap(value, stride_a), swap(value, stride_b))
        tables.append(value)
    top = functools.reduce(jnp.maximum, [t[0:1] for t in tables])
    total = sum(t[1:2] * jnp.exp(t[0:1] - top) for t in tables)
    picked = sum(t[2:3] for t in tables)
    out_ref[0:8, :] = jnp.zeros((8, tokens), jnp.float32)
    if final:
        out_ref[0:1, :] = top + jnp.log(total)
        out_ref[1:2, :] = picked
        out_ref[8:, :] = refs[count][...]
    else:
        out_ref[0:1, :] = top
        out_ref[1:2, :] = total
        out_ref[2:3, :] = picked


def run_merge(weights, table, arrived, lanes, tops):
    operands = [table, *arrived] + ([] if tops is None else [tops]) + [weights]
    rows = 8 + (0 if tops is None else tops.shape[0])
    return pl.pallas_call(
        functools.partial(merge_kernel, len(arrived), lanes, tops is not None),
        in_specs=[whole_vmem()] * len(operands),
        out_specs=whole_vmem(),
        out_shape=jax.ShapeDtypeStruct((rows, table.shape[1]), jnp.float32),
        compiler_params=pltpu.CompilerParams(vmem_limit_bytes=VMEM_SHARED),
        cost_estimate=SMALL,
        name="totals",
    )(*operands)


def logits_kernel(
    tile, tiles, group_index, rows_a_ref, rows_b_ref, gain_ref, labels_ref, w_ref, *refs
):
    p_ref, l_ref, normed_ref, tops_ref, stats_ref, even_ref, odd_ref, m_ref, s_ref, picked_ref = refs[-10:]
    logits_refs = even_ref, odd_ref
    step = pl.program_id(0)
    tokens = normed_ref.shape[0]
    last_rows = w_ref.shape[0] - (tiles - 1) * tile

    def matmul(slot, start, rows):
        def piece(place, size):
            def work():
                logits_refs[slot][place : place + size, :] = lax.dot_general(
                    w_ref[pl.ds(start + place, size), :], normed_ref[...], (((1,), (1,)), ((), ())),
                    preferred_element_type=jnp.float32,
                )

            return work

        return [piece(place, min(PIECE, rows - place)) for place in range(0, rows, PIECE)]

    def soften(slot, index, valid_rows):
        group = min(tokens, LANES)
        items = []
        for col in range(0, tokens, group):
            state = {}
            cols = slice(col, col + group)
            target = labels_ref[:, group_index * tokens + col : group_index * tokens + col + group] - index * tile

            def find_top(cols=cols, state=state):
                top = None
                for start, rows in chunks(valid_rows):
                    part = jnp.max(logits_refs[slot][start : start + rows, cols], axis=0, keepdims=True)
                    top = part if top is None else jnp.maximum(top, part)
                state.update(top=top, total=jnp.zeros((1, group), jnp.float32), picked=picked_ref[:, cols])

            def chunk(start, rows, cols=cols, state=state, target=target):
                values = logits_refs[slot][start : start + rows, cols]
                row = lax.broadcasted_iota(jnp.int32, (rows, group), 0)
                lowered = values - state["top"]
                exps = jnp.exp(lowered)
                l_ref[start : start + rows, cols] = lowered.astype(l_ref.dtype)
                p_ref[start : start + rows, cols] = exps.astype(p_ref.dtype)
                chosen = jnp.where(row == target - start, values, 0.0)
                state["total"] = state["total"] + jnp.sum(exps, axis=0, keepdims=True)
                state["picked"] = state["picked"] + jnp.sum(chosen, axis=0, keepdims=True)

            def finish(cols=cols, state=state):
                here = lax.broadcasted_iota(jnp.int32, (m_ref.shape[0], group), 0) == index
                m_ref[:, cols] = jnp.where(here, state["top"], m_ref[:, cols])
                s_ref[:, cols] = jnp.where(here, state["total"], s_ref[:, cols])
                picked_ref[:, cols] = state["picked"]

            items.append(find_top)
            items += [functools.partial(chunk, start, rows) for start, rows in chunks(valid_rows)]
            items.append(finish)
        return items

    @pl.when(step == 0)
    def _():
        half = tokens // 2
        for place, rows_ref in ((0, rows_a_ref), (half, rows_b_ref)):
            values = rows_ref[...].astype(jnp.float32)
            inverse = lax.rsqrt(jnp.mean(values * values, axis=-1, keepdims=True) + EPS)
            normed_ref[place : place + half, :] = (values * inverse * gain_ref[...]).astype(jnp.bfloat16)
        m_ref[...] = jnp.full_like(m_ref, -jnp.inf)
        s_ref[...] = jnp.zeros_like(s_ref)
        picked_ref[...] = jnp.zeros_like(picked_ref)
        together(matmul(0, 0, last_rows if tiles == 1 else tile), [])

    if tiles > 2:

        for parity in range(2):

            @pl.when((step > 0) & (step < tiles - 1) & (lax.rem(step, 2) == parity))
            def _(parity=parity):
                together(matmul(parity, pl.multiple_of(step * tile, tile), tile), soften(1 - parity, step - 1, tile))

    if tiles > 1:

        @pl.when(step == tiles - 1)
        def _():
            together(matmul((tiles - 1) % 2, (tiles - 1) * tile, last_rows), soften(tiles % 2, tiles - 2, tile))

    @pl.when(step == tiles)
    def _():
        together([], soften((tiles - 1) % 2, tiles - 1, last_rows))
        tops = m_ref[...]
        top = jnp.max(tops, axis=0, keepdims=True)
        total = jnp.sum(s_ref[...] * jnp.exp(tops - top), axis=0, keepdims=True)
        place = group_index * tokens
        cols = slice(place, place + tokens)
        if group_index:
            stats_ref[:, :place] = refs[1][...]
            tops_ref[:, :place] = refs[2][...]
        tops_ref[:, cols] = tops
        stats_ref[:, cols] = jnp.zeros((8, tokens), jnp.float32)
        stats_ref[0:1, cols] = top
        stats_ref[1:2, cols] = total
        stats_ref[2:3, cols] = picked_ref[...]


def run_logits(group, rows_a, rows_b, gain, labels, weights, before):
    half, width = rows_a.shape
    tokens = 2 * half
    vocab_dev = weights.shape[0]
    tile, tiles = tiling(vocab_dev, TILE)
    groups = cdiv(tiles, 8) * 8
    behind = pl.BlockSpec((tile, tokens), lambda j: (jnp.maximum(j - 1, 0), 0))
    operands = [rows_a, rows_b, gain, labels, weights]
    in_specs = [
        whole_vmem(),
        whole_vmem(),
        whole((1, width)),
        whole_vmem(),
        whole_vmem(),
    ]
    aliases = {}
    if group:
        aliases[len(operands)] = 2
        operands += before
        in_specs += [pl.BlockSpec(memory_space=pl.ANY), whole_vmem(), whole_vmem()]
    return pl.pallas_call(
        functools.partial(logits_kernel, tile, tiles, group),
        grid=(tiles + 1,),
        in_specs=in_specs,
        out_specs=[
            behind,
            behind,
            pl.BlockSpec((tokens, width), lambda j: (group, 0)),
            whole_vmem(),
            whole_vmem(),
        ],
        out_shape=[
            jax.ShapeDtypeStruct((vocab_dev, tokens), jnp.bfloat16),
            jax.ShapeDtypeStruct((vocab_dev, tokens), jnp.bfloat16),
            jax.ShapeDtypeStruct((2 * tokens, width), jnp.bfloat16),
            jax.ShapeDtypeStruct((groups, (group + 1) * tokens), jnp.float32),
            jax.ShapeDtypeStruct((8, (group + 1) * tokens), jnp.float32),
        ],
        scratch_shapes=[
            pltpu.VMEM((tile, tokens), jnp.float32),
            pltpu.VMEM((tile, tokens), jnp.float32),
            pltpu.VMEM((groups, tokens), jnp.float32),
            pltpu.VMEM((groups, tokens), jnp.float32),
            pltpu.VMEM((1, tokens), jnp.float32),
        ],
        input_output_aliases=aliases,
        compiler_params=pltpu.CompilerParams(vmem_limit_bytes=VMEM_SHARED),
        cost_estimate=pl.CostEstimate(
            flops=2 * tokens * width * vocab_dev,
            bytes_accessed=4 * tokens * vocab_dev,
            transcendentals=tokens * vocab_dev,
        ),
        name="logits",
    )(*operands)


def dlogits_kernel(
    tile, tiles, group_index, own_ref, other_ref, labels_ref, ps_ref, pt_ref, l_ref, w_ref, *refs
):
    d_ref, first_ref, second_ref, up_ref, even_ref, odd_ref, a_ref, b_ref, g_ref, c_ref = refs[-10:]
    d_refs = even_ref, odd_ref
    step = pl.program_id(0)
    tokens = ps_ref.shape[1]
    all_tokens = labels_ref.shape[1]
    first = group_index * tokens
    scale = 1.0 / all_tokens
    last_rows = w_ref.shape[0] - (tiles - 1) * tile

    def weigh(slot, index, valid_rows):
        group = min(tokens, LANES)
        items = []
        for col in range(0, tokens, group):
            state = {}
            cols = slice(col, col + group)
            target = labels_ref[:, first + col : first + col + group] - index * tile

            def begin(cols=cols, state=state):
                state.update(
                    own=pick_row(a_ref[:, cols], index),
                    other=pick_row(b_ref[:, cols], index),
                    gap=pick_row(g_ref[:, cols], index),
                    cross=c_ref[:, cols],
                )

            def chunk(start, rows, cols=cols, state=state, target=target):
                here = slice(start, start + rows)
                row = lax.broadcasted_iota(jnp.int32, (rows, group), 0)
                student = ps_ref[here, cols].astype(jnp.float32) * state["own"]
                teacher = pt_ref[here, cols].astype(jnp.float32) * state["other"]
                lowered = l_ref[here, cols].astype(jnp.float32)
                part = teacher * (state["gap"] - lowered)
                value = student - teacher - jnp.where(row == target - start, scale, 0.0)
                state["cross"] = state["cross"] + jnp.sum(part, axis=0, keepdims=True)
                value = value.astype(jnp.bfloat16)
                d_ref[here, cols] = value
                d_refs[slot][here, cols] = value

            def finish(cols=cols, state=state):
                c_ref[:, cols] = state["cross"]

            items.append(begin)
            items += [functools.partial(chunk, start, rows) for start, rows in chunks(valid_rows)]
            items.append(finish)
        return items

    def matmul(slot, start, rows):
        def piece(out):
            def work():
                cols = slice(out, out + PIECE)
                up_ref[:, cols] += lax.dot_general(
                    d_refs[slot][:rows, :], w_ref[pl.ds(start, rows), cols], (((0,), (0,)), ((), ())),
                    preferred_element_type=jnp.float32,
                )

            return work

        return [piece(out) for out in range(0, up_ref.shape[1], PIECE)]

    @pl.when(step == 0)
    def _():
        here = slice(first, first + tokens)
        own_total, other_total = own_ref[0:1, here], other_ref[0:1, here]
        a_ref[...] = jnp.exp(own_ref[8:, here] - own_total) * ((1.0 + BETA) * scale)
        b_ref[...] = jnp.exp(other_ref[8:, here] - other_total) * (BETA * scale)
        g_ref[...] = own_total - own_ref[8:, here]
        c_ref[...] = jnp.zeros_like(c_ref)
        up_ref[...] = jnp.zeros_like(up_ref)
        together([], weigh(0, 0, last_rows if tiles == 1 else tile))

    if tiles > 2:

        for parity in range(2):

            @pl.when((step > 0) & (step < tiles - 1) & (lax.rem(step, 2) == parity))
            def _(parity=parity):
                together(matmul(1 - parity, pl.multiple_of((step - 1) * tile, tile), tile), weigh(parity, step, tile))

    if tiles > 1:

        @pl.when(step == tiles - 1)
        def _():
            together(matmul(tiles % 2, (tiles - 2) * tile, tile), weigh((tiles - 1) % 2, tiles - 1, last_rows))

    @pl.when(step == tiles)
    def _():
        together(matmul((tiles - 1) % 2, (tiles - 1) * tile, last_rows), [])
        width = up_ref.shape[1]
        half = tokens // 2
        column = jnp.broadcast_to(c_ref[...] * (all_tokens / BETA), (LANES, tokens)).T
        lane = lax.broadcasted_iota(jnp.int32, (tokens, LANES), 1)
        if first_ref.dtype == jnp.float32:
            edge = jnp.where(lane == 0, column, 0.0)
        else:
            high = column.astype(jnp.bfloat16).astype(jnp.float32)
            edge = jnp.where(lane == 0, high, jnp.where(lane == 1, column - high, 0.0))
        for ref, place in ((first_ref, 0), (second_ref, half)):
            ref[:, :width] = up_ref[place : place + half, :].astype(ref.dtype)
            ref[:, width:] = edge[place : place + half, :].astype(ref.dtype)


def run_dlogits(group, totals, other_totals, labels, p_own, p_other, lowered, weights, dlogits, out_type):
    tokens = p_own.shape[1]
    vocab_dev, width = weights.shape
    tile, tiles = tiling(vocab_dev, TILE)
    groups = totals.shape[0] - 8
    wide = width + LANES
    ahead = lambda j: jnp.minimum(j, tiles - 1)
    here = pl.BlockSpec((tile, tokens), lambda j: (ahead(j), 0))
    p_own, p_other, lowered = (pltpu.with_memory_space_constraint(v, pltpu.HBM) for v in (p_own, p_other, lowered))
    operands = [totals, other_totals, labels, p_own, p_other, lowered, weights]
    in_specs = [
        whole_vmem(),
        whole_vmem(),
        whole_vmem(),
        here,
        here,
        here,
        pl.BlockSpec(memory_space=pltpu.VMEM),
    ]
    aliases = {}
    if dlogits is not None:
        aliases[len(operands)] = 0
        operands.append(dlogits)
        in_specs.append(pl.BlockSpec(memory_space=pl.ANY))
    return pl.pallas_call(
        functools.partial(dlogits_kernel, tile, tiles, group),
        grid=(tiles + 1,),
        in_specs=in_specs,
        out_specs=[
            pl.BlockSpec((tile, tokens), lambda j: (ahead(j), group)),
            whole_vmem(),
            whole_vmem(),
        ],
        out_shape=[
            jax.ShapeDtypeStruct((vocab_dev, 2 * tokens), jnp.bfloat16),
            jax.ShapeDtypeStruct((tokens // 2, wide), out_type),
            jax.ShapeDtypeStruct((tokens // 2, wide), out_type),
        ],
        scratch_shapes=[
            pltpu.VMEM((tokens, width), jnp.float32),
            pltpu.VMEM((tile, tokens), jnp.bfloat16),
            pltpu.VMEM((tile, tokens), jnp.bfloat16),
            pltpu.VMEM((groups, tokens), jnp.float32),
            pltpu.VMEM((groups, tokens), jnp.float32),
            pltpu.VMEM((groups, tokens), jnp.float32),
            pltpu.VMEM((1, tokens), jnp.float32),
        ],
        input_output_aliases=aliases,
        compiler_params=pltpu.CompilerParams(vmem_limit_bytes=VMEM_SHARED),
        cost_estimate=pl.CostEstimate(
            flops=2 * tokens * width * vocab_dev,
            bytes_accessed=8 * tokens * vocab_dev,
            transcendentals=0,
        ),
        name="dlogits",
    )(*operands)


def fold_kernel(count, gots, sends, *refs):
    sums, arrived, outs = refs[:count], refs[count : count + gots], refs[-1 - sends :]
    keep, send = outs[0], outs[1:]
    width = keep.shape[2] - LANES
    cut = keep.shape[1]
    lane = lax.broadcasted_iota(jnp.int32, (cut, LANES), 1)
    for part in range(2):
        held = sums[part][...] if count == 2 else sums[0][part]
        got = arrived[part][...] if gots == 2 else arrived[0][part]
        total = held + got.astype(jnp.float32)
        keep[part] = total[:cut]
        gone = total[cut:]
        cross = gone[:, width : width + 1] + gone[:, width + 1 : width + 2]
        high = cross.astype(jnp.bfloat16).astype(jnp.float32)
        edge = jnp.where(lane == 0, high, jnp.where(lane == 1, cross - high, 0.0))
        value = jnp.concatenate([gone[:, :width], edge], axis=1).astype(jnp.bfloat16)
        if sends == 2:
            send[part][...] = value
        else:
            send[0][part] = value


def run_fold(sums, arrived, sends, after):
    rows, wide = sums[0].shape[-2:]
    cut = rows // 2
    operands = list(sums) + list(arrived)
    in_specs = [pl.BlockSpec(memory_space=pltpu.VMEM)] * len(operands)
    if after is not None:
        operands.append(pltpu.with_memory_space_constraint(after, pltpu.HBM))
        in_specs.append(pl.BlockSpec(memory_space=pl.ANY))
    shape = (cut, wide) if sends == 2 else (2, cut, wide)
    return pl.pallas_call(
        functools.partial(fold_kernel, len(sums), len(arrived), sends),
        in_specs=in_specs,
        out_specs=[pl.BlockSpec(memory_space=pltpu.VMEM)] * (1 + sends),
        out_shape=[jax.ShapeDtypeStruct((2, cut, wide), jnp.float32)]
        + [jax.ShapeDtypeStruct(shape, jnp.bfloat16)] * sends,
        compiler_params=pltpu.CompilerParams(vmem_limit_bytes=VMEM_SHARED),
        cost_estimate=SMALL,
        name="fold",
    )(*operands)


def head_grad_kernel(normed_ref, d_ref, *refs):
    out_ref = refs[-1]
    out_ref[...] = jnp.dot(d_ref[...], normed_ref[...], preferred_element_type=jnp.float32).astype(out_ref.dtype)


def run_head_grad(first, count, normed, dlogits, grad, after):
    tokens, width = normed.shape
    vocab_dev = dlogits.shape[0]
    tile, tiles = tiling(vocab_dev, GRAD_TILE)
    operands = [normed, pltpu.with_memory_space_constraint(dlogits, pltpu.HBM)]
    in_specs = [whole((tokens, width)), pl.BlockSpec((tile, tokens), lambda j: (first + j, 0))]
    aliases = {}
    for value in after:
        operands.append(value)
        in_specs.append(pl.BlockSpec(memory_space=pl.ANY))
    if grad is not None:
        aliases[len(operands)] = 0
        operands.append(pltpu.with_memory_space_constraint(grad, pltpu.HBM))
        in_specs.append(pl.BlockSpec(memory_space=pl.ANY))
    return pl.pallas_call(
        head_grad_kernel,
        grid=(count,),
        in_specs=in_specs,
        out_specs=pl.BlockSpec((tile, width), lambda j: (first + j, 0)),
        out_shape=jax.ShapeDtypeStruct((vocab_dev, width), jnp.bfloat16),
        input_output_aliases=aliases,
        compiler_params=pltpu.CompilerParams(vmem_limit_bytes=VMEM_ALONE),
        cost_estimate=pl.CostEstimate(
            flops=2 * tokens * width * tile * count,
            bytes_accessed=2 * width * tile * count + 2 * tokens * tile * count,
            transcendentals=0,
        ),
        name="head_grad",
    )(*operands)


def moved(value, offset):
    n = lax.axis_size("fsdp")
    return lax.ppermute(value, "fsdp", [(i, i ^ offset) for i in range(n)])


def other_member(value):
    return lax.ppermute(value, "member", [(0, 1), (1, 0)])


def token_order(bits):
    offsets = [0]
    for bit in reversed(range(2, bits)):
        offsets = offsets + [o | 1 << bit for o in offsets]
    order = []
    for group in range(2):
        for half in range(2):
            group_bit, place_bit = (1, 2) if half == 0 else (2, 1)
            for place in range(2):
                order += [(group * group_bit + place * place_bit + o, half) for o in offsets]
    return order


def lane_moves(offset, bits, half):
    moves = []
    for bit in range(bits):
        if offset >> bit & 1:
            group, place = half << bits, half << (bits - 2)
            strides = {0: (group, place), 1: (place, group)}.get(bit, (half << (bits - 1 - bit),) * 2)
            moves.append(strides + (half << (bits - 1),))
    return tuple(moves)


def pack(value, width):
    cross = value[..., width : width + 1] + value[..., width + 1 : width + 2]
    high = lax.reduce_precision(cross, 8, 7)
    rest = jnp.zeros(value.shape[:-1] + (LANES - 2,), jnp.float32)
    return jnp.concatenate([value[..., :width], high, cross - high, rest], axis=-1).astype(jnp.bfloat16)


def body(hidden, gain, head, labels):
    own_rows = hidden[0]
    gain_row = gain[0]
    tok_dev, width = own_rows.shape
    vocab_dev = head.shape[2]
    count = lax.axis_size("fsdp")
    bits = count.bit_length() - 1
    index = lax.axis_index("fsdp")
    half = tok_dev // 2
    tokens = tok_dev * count

    order = token_order(bits)
    offsets = jnp.asarray([o for o, _ in order], jnp.int32)
    halves = jnp.asarray([s for _, s in order], jnp.int32)
    local_labels = labels.reshape(2 * count, half)[(offsets ^ index) * 2 + halves].reshape(1, tokens)
    local_labels = local_labels - index * vocab_dev

    first_rows = min(vocab_dev, cdiv(vocab_dev // 2, 16) * 16)
    weights = pinned(run_load(0, first_rows, head[0].T, local_labels, None))
    held = [own_rows]
    for bit in reversed(range(2, bits)):
        held = run_join([held[0], moved(held[0], 1 << bit)], bit == 2, weights)
        if bit == bits - 1 and first_rows < vocab_dev:
            weights = pinned(run_load(first_rows, vocab_dev - first_rows, head[0].T, held[0], weights))
    near_a, near_b = run_stack(weights, held[0], moved(held[0], 2), held[1], moved(held[1], 1))
    far_a = moved(near_a, 1)
    far_b = moved(near_b, 2)

    p_near, l_near, normed, tops, stats = run_logits(
        0, near_a, near_b, gain_row[None], local_labels, weights, []
    )
    p_near_other = other_member(p_near)
    p_far, l_far, normed, tops, table = run_logits(
        1, far_a, far_b, gain_row[None], local_labels, weights, [normed, stats, tops]
    )
    p_far_other = other_member(p_far)

    for bit in range(0, bits, 2):
        steps = [k << bit for k in range(1, 4) if k << bit < count]
        lanes = [lane_moves(k, bits, half) for k in steps]
        table = run_merge(weights, table, [moved(table, k) for k in steps], lanes, tops if bit + 2 >= bits else None)
    other_totals = other_member(table)

    dlogits, send_a, send_b = run_dlogits(
        1, table, other_totals, local_labels, p_far, p_far_other, l_far, weights, None, jnp.bfloat16
    )
    got_a, got_b = moved(send_a, 1), moved(send_b, 2)
    dlogits, sum_a, sum_b = run_dlogits(
        0, table, other_totals, local_labels, p_near, p_near_other, l_near, weights, dlogits, jnp.float32
    )

    tile, tiles = tiling(vocab_dev, GRAD_TILE)
    edges = [tiles * i // 8 for i in GRAD_EDGES]
    grad = None
    summed, sends = run_fold((sum_a, sum_b), (got_a, got_b), 2, None), 2
    for step in range(1, bits):
        keep, send = summed[0], summed[1:]
        if step <= 3 and edges[step] > edges[step - 1]:
            grad = run_head_grad(edges[step - 1], edges[step] - edges[step - 1], normed, dlogits, grad, send)
        if step == 1:
            got = [moved(send[0], 2), moved(send[1], 1)]
        else:
            got = [moved(send[0], 1 << step)]
        cut = keep.shape[1] // 2
        if step < bits - 1 and cut % 16 == 0:
            summed = run_fold((keep,), got, 1, grad)
        else:
            total = keep + (jnp.stack(got) if step == 1 else got[0]).astype(jnp.float32)
            if step < bits - 1:
                summed = [total[:, :cut], pack(total[:, cut:], width)]
            else:
                summed = total
    summed = summed.reshape(tok_dev, -1)
    cross = summed[:, width] + summed[:, width + 1]
    summed = summed[:, :width]

    quarter = tokens // 4
    own = lambda row: jnp.concatenate([row[:half], row[quarter : quarter + half]])
    token_loss = own(table[0]) - own(table[1]) + BETA * cross
    values = own_rows.astype(jnp.float32)
    inverse = lax.rsqrt(jnp.mean(values * values, axis=-1, keepdims=True) + EPS)
    scaled = gain_row * summed
    inner = jnp.mean(scaled * values, axis=-1, keepdims=True)
    hidden_grad = inverse * scaled - values * inverse**3 * inner
    return (token_loss[None], grad.T[None], hidden_grad.astype(jnp.bfloat16)[None])


def solution(mesh):
    in_specs = (P("member", "fsdp", None), P("member", None), P("member", None, "fsdp"), P())
    out_specs = (P("member", "fsdp"), P("member", None, "fsdp"), P("member", "fsdp", None))
    return jax.shard_map(body, mesh=mesh, in_specs=in_specs, out_specs=out_specs, check_vma=False)
```

```python
import functools
import jax
import jax.numpy as jnp
from jax import lax
from jax.experimental import pallas as pl
from jax.experimental.pallas import tpu as pltpu
from jax.sharding import PartitionSpec as P

EPS = 1e-05
BETA = 0.5
TILE = 1024
GRAD_TILE = 1024
CHUNK = 128
PIECE = 512
LANES = 128
VMEM_SHARED = 34200000
VMEM_ALONE = 40 * 1024 * 1024
GRAD_EDGES = (0, 3, 5, 8)
LOAD_COPIES = 4
SMALL = pl.CostEstimate(flops=4096, bytes_accessed=4096, transcendentals=0)


def cdiv(a, b):
    return -(-a // b)


def tiling(vocab_dev, tile):
    tile = min(tile, vocab_dev)
    return tile, cdiv(vocab_dev, tile)


def whole(shape):
    return pl.BlockSpec(shape, lambda j: (0, 0))


def whole_vmem():
    return pl.BlockSpec(memory_space=pltpu.VMEM)


def together(first, second):
    done = 0
    for i, work in enumerate(first):
        work()
        upto = len(second) * (i + 1) // len(first)
        for other in second[done:upto]:
            other()
        done = upto
    if not first:
        for other in second:
            other()


def pinned(value):
    return pltpu.with_memory_space_constraint(value, pltpu.VMEM)


def chunks(valid):
    return [(start, min(CHUNK, valid - start)) for start in range(0, valid, CHUNK)]


def pick_row(table, index):
    here = lax.broadcasted_iota(jnp.int32, table.shape, 0) == index
    return jnp.sum(jnp.where(here, table, 0.0), axis=0, keepdims=True)


def load_kernel(first, rows, w_ref, *refs):
    out_ref, sems = refs[-2:]
    pieces = []
    step = cdiv(cdiv(rows, LOAD_COPIES), 16) * 16
    for i, start in enumerate(range(0, rows, step)):
        piece = pl.ds(first + start, min(step, rows - start))
        pieces.append(pltpu.make_async_copy(w_ref.at[piece, :], out_ref.at[piece, :], sems.at[i]))
    for piece in pieces:
        piece.start()
    for piece in pieces:
        piece.wait()


def run_load(first, rows, weights, after, held):
    operands, in_specs, aliases = [weights, after], [pl.BlockSpec(memory_space=pl.ANY)] * 2, {}
    if held is not None:
        operands.append(held)
        in_specs.append(whole_vmem())
        aliases[2] = 0
    return pl.pallas_call(
        functools.partial(load_kernel, first, rows),
        in_specs=in_specs,
        out_specs=whole_vmem(),
        out_shape=pltpu.VMEM(weights.shape, weights.dtype),
        scratch_shapes=[pltpu.SemaphoreType.DMA((LOAD_COPIES,))],
        input_output_aliases=aliases,
        compiler_params=pltpu.CompilerParams(vmem_limit_bytes=VMEM_SHARED),
        cost_estimate=pl.CostEstimate(flops=0, bytes_accessed=4 * rows * weights.shape[1], transcendentals=0),
        name="load",
    )(*operands)


def join_kernel(count, split, *refs):
    pieces, outs = refs[:count], refs[-2 if split else -1 :]
    for i, piece in enumerate(pieces):
        half = piece.shape[0] // 2
        for part in range(2):
            rows = piece[part * half : (part + 1) * half, :]
            if split:
                outs[part][i * half : (i + 1) * half, :] = rows
            else:
                place = (part * count + i) * half
                outs[0][place : place + half, :] = rows


def run_join(pieces, split, weights):
    rows, width = pieces[0].shape
    total = rows * len(pieces)
    kind = lambda n: jax.ShapeDtypeStruct((n, width), pieces[0].dtype)
    return pl.pallas_call(
        functools.partial(join_kernel, len(pieces), split),
        in_specs=[whole_vmem()] * (len(pieces) + 1),
        out_specs=[whole_vmem()] * (2 if split else 1),
        out_shape=[kind(total // 2)] * 2 if split else [kind(total)],
        compiler_params=pltpu.CompilerParams(vmem_limit_bytes=VMEM_SHARED),
        cost_estimate=SMALL,
        name="join",
    )(*pieces, weights)


def stack_kernel(w_ref, low_a, high_a, low_b, high_b, a_ref, b_ref):
    half = low_a.shape[0]
    for low, high, out in ((low_a, high_a, a_ref), (low_b, high_b, b_ref)):
        out[:half, :] = low[...]
        out[half:, :] = high[...]


def run_stack(weights, *pieces):
    rows, width = pieces[0].shape
    return pl.pallas_call(
        stack_kernel,
        in_specs=[whole_vmem()] * 5,
        out_specs=[whole_vmem()] * 2,
        out_shape=[jax.ShapeDtypeStruct((2 * rows, width), pieces[0].dtype)] * 2,
        cost_estimate=SMALL,
        compiler_params=pltpu.CompilerParams(vmem_limit_bytes=VMEM_SHARED),
        name="stack",
    )(weights, *pieces)


def merge_kernel(count, lanes, final, table_ref, *refs):
    arrived, out_ref = refs[:count], refs[-1]
    tokens = table_ref.shape[1]
    lane = lax.broadcasted_iota(jnp.int32, (8, tokens), 1)

    def swap(value, stride):
        return jnp.where(
            lane & stride == 0, pltpu.roll(value, tokens - stride, 1), pltpu.roll(value, stride, 1)
        )

    tables = [table_ref[...]]
    for ref, moves in zip(arrived, lanes):
        value = ref[...]
        for stride_a, stride_b, part in moves:
            if stride_a == stride_b:
                value = swap(value, stride_a)
            else:
                value = jnp.where(lane & part == 0, swap(value, stride_a), swap(value, stride_b))
        tables.append(value)
    top = functools.reduce(jnp.maximum, [t[0:1] for t in tables])
    total = sum(t[1:2] * jnp.exp(t[0:1] - top) for t in tables)
    picked = sum(t[2:3] for t in tables)
    out_ref[0:8, :] = jnp.zeros((8, tokens), jnp.float32)
    if final:
        out_ref[0:1, :] = top + jnp.log(total)
        out_ref[1:2, :] = picked
        out_ref[8:, :] = refs[count][...]
    else:
        out_ref[0:1, :] = top
        out_ref[1:2, :] = total
        out_ref[2:3, :] = picked


def run_merge(weights, table, arrived, lanes, tops):
    operands = [table, *arrived] + ([] if tops is None else [tops]) + [weights]
    rows = 8 + (0 if tops is None else tops.shape[0])
    return pl.pallas_call(
        functools.partial(merge_kernel, len(arrived), lanes, tops is not None),
        in_specs=[whole_vmem()] * len(operands),
        out_specs=whole_vmem(),
        out_shape=jax.ShapeDtypeStruct((rows, table.shape[1]), jnp.float32),
        compiler_params=pltpu.CompilerParams(vmem_limit_bytes=VMEM_SHARED),
        cost_estimate=SMALL,
        name="totals",
    )(*operands)


def logits_kernel(
    tile, tiles, group_index, rows_a_ref, rows_b_ref, gain_ref, labels_ref, w_ref, *refs
):
    p_ref, l_ref, normed_ref, tops_ref, stats_ref, even_ref, odd_ref, m_ref, s_ref, picked_ref = refs[-10:]
    logits_refs = even_ref, odd_ref
    step = pl.program_id(0)
    tokens = normed_ref.shape[0]
    last_rows = w_ref.shape[0] - (tiles - 1) * tile

    def matmul(slot, start, rows):
        def piece(place, size):
            def work():
                logits_refs[slot][place : place + size, :] = lax.dot_general(
                    w_ref[pl.ds(start + place, size), :], normed_ref[...], (((1,), (1,)), ((), ())),
                    preferred_element_type=jnp.float32,
                )

            return work

        return [piece(place, min(PIECE, rows - place)) for place in range(0, rows, PIECE)]

    def soften(slot, index, valid_rows):
        group = min(tokens, LANES)
        items = []
        for col in range(0, tokens, group):
            state = {}
            cols = slice(col, col + group)
            target = labels_ref[:, group_index * tokens + col : group_index * tokens + col + group] - index * tile

            def find_top(cols=cols, state=state):
                top = None
                for start, rows in chunks(valid_rows):
                    part = jnp.max(logits_refs[slot][start : start + rows, cols], axis=0, keepdims=True)
                    top = part if top is None else jnp.maximum(top, part)
                state.update(top=top, total=jnp.zeros((1, group), jnp.float32), picked=picked_ref[:, cols])

            def chunk(start, rows, cols=cols, state=state, target=target):
                values = logits_refs[slot][start : start + rows, cols]
                row = lax.broadcasted_iota(jnp.int32, (rows, group), 0)
                lowered = values - state["top"]
                exps = jnp.exp(lowered)
                l_ref[start : start + rows, cols] = lowered.astype(l_ref.dtype)
                p_ref[start : start + rows, cols] = exps.astype(p_ref.dtype)
                chosen = jnp.where(row == target - start, values, 0.0)
                state["total"] = state["total"] + jnp.sum(exps, axis=0, keepdims=True)
                state["picked"] = state["picked"] + jnp.sum(chosen, axis=0, keepdims=True)

            def finish(cols=cols, state=state):
                here = lax.broadcasted_iota(jnp.int32, (m_ref.shape[0], group), 0) == index
                m_ref[:, cols] = jnp.where(here, state["top"], m_ref[:, cols])
                s_ref[:, cols] = jnp.where(here, state["total"], s_ref[:, cols])
                picked_ref[:, cols] = state["picked"]

            items.append(find_top)
            items += [functools.partial(chunk, start, rows) for start, rows in chunks(valid_rows)]
            items.append(finish)
        return items

    @pl.when(step == 0)
    def _():
        half = tokens // 2
        for place, rows_ref in ((0, rows_a_ref), (half, rows_b_ref)):
            values = rows_ref[...].astype(jnp.float32)
            inverse = lax.rsqrt(jnp.mean(values * values, axis=-1, keepdims=True) + EPS)
            normed_ref[place : place + half, :] = (values * inverse * gain_ref[...]).astype(jnp.bfloat16)
        m_ref[...] = jnp.full_like(m_ref, -jnp.inf)
        s_ref[...] = jnp.zeros_like(s_ref)
        picked_ref[...] = jnp.zeros_like(picked_ref)
        together(matmul(0, 0, last_rows if tiles == 1 else tile), [])

    if tiles > 2:

        for parity in range(2):

            @pl.when((step > 0) & (step < tiles - 1) & (lax.rem(step, 2) == parity))
            def _(parity=parity):
                together(matmul(parity, pl.multiple_of(step * tile, tile), tile), soften(1 - parity, step - 1, tile))

    if tiles > 1:

        @pl.when(step == tiles - 1)
        def _():
            together(matmul((tiles - 1) % 2, (tiles - 1) * tile, last_rows), soften(tiles % 2, tiles - 2, tile))

    @pl.when(step == tiles)
    def _():
        together([], soften((tiles - 1) % 2, tiles - 1, last_rows))
        tops = m_ref[...]
        top = jnp.max(tops, axis=0, keepdims=True)
        total = jnp.sum(s_ref[...] * jnp.exp(tops - top), axis=0, keepdims=True)
        place = group_index * tokens
        cols = slice(place, place + tokens)
        if group_index:
            stats_ref[:, :place] = refs[1][...]
            tops_ref[:, :place] = refs[2][...]
        tops_ref[:, cols] = tops
        stats_ref[:, cols] = jnp.zeros((8, tokens), jnp.float32)
        stats_ref[0:1, cols] = top
        stats_ref[1:2, cols] = total
        stats_ref[2:3, cols] = picked_ref[...]


def run_logits(group, rows_a, rows_b, gain, labels, weights, before):
    half, width = rows_a.shape
    tokens = 2 * half
    vocab_dev = weights.shape[0]
    tile, tiles = tiling(vocab_dev, TILE)
    groups = cdiv(tiles, 8) * 8
    behind = pl.BlockSpec((tile, tokens), lambda j: (jnp.maximum(j - 1, 0), 0))
    operands = [rows_a, rows_b, gain, labels, weights]
    in_specs = [
        whole_vmem(),
        whole_vmem(),
        whole((1, width)),
        whole_vmem(),
        whole_vmem(),
    ]
    aliases = {}
    if group:
        aliases[len(operands)] = 2
        operands += before
        in_specs += [pl.BlockSpec(memory_space=pl.ANY), whole_vmem(), whole_vmem()]
    return pl.pallas_call(
        functools.partial(logits_kernel, tile, tiles, group),
        grid=(tiles + 1,),
        in_specs=in_specs,
        out_specs=[
            behind,
            behind,
            pl.BlockSpec((tokens, width), lambda j: (group, 0)),
            whole_vmem(),
            whole_vmem(),
        ],
        out_shape=[
            jax.ShapeDtypeStruct((vocab_dev, tokens), jnp.bfloat16),
            jax.ShapeDtypeStruct((vocab_dev, tokens), jnp.bfloat16),
            jax.ShapeDtypeStruct((2 * tokens, width), jnp.bfloat16),
            jax.ShapeDtypeStruct((groups, (group + 1) * tokens), jnp.float32),
            jax.ShapeDtypeStruct((8, (group + 1) * tokens), jnp.float32),
        ],
        scratch_shapes=[
            pltpu.VMEM((tile, tokens), jnp.float32),
            pltpu.VMEM((tile, tokens), jnp.float32),
            pltpu.VMEM((groups, tokens), jnp.float32),
            pltpu.VMEM((groups, tokens), jnp.float32),
            pltpu.VMEM((1, tokens), jnp.float32),
        ],
        input_output_aliases=aliases,
        compiler_params=pltpu.CompilerParams(vmem_limit_bytes=VMEM_SHARED),
        cost_estimate=pl.CostEstimate(
            flops=2 * tokens * width * vocab_dev,
            bytes_accessed=4 * tokens * vocab_dev,
            transcendentals=tokens * vocab_dev,
        ),
        name="logits",
    )(*operands)


def dlogits_kernel(
    tile, tiles, group_index, own_ref, other_ref, labels_ref, ps_ref, pt_ref, l_ref, w_ref, *refs
):
    d_ref, first_ref, second_ref, up_ref, even_ref, odd_ref, a_ref, b_ref, g_ref, c_ref = refs[-10:]
    d_refs = even_ref, odd_ref
    step = pl.program_id(0)
    tokens = ps_ref.shape[1]
    all_tokens = labels_ref.shape[1]
    first = group_index * tokens
    scale = 1.0 / all_tokens
    last_rows = w_ref.shape[0] - (tiles - 1) * tile

    def weigh(slot, index, valid_rows):
        group = min(tokens, LANES)
        items = []
        for col in range(0, tokens, group):
            state = {}
            cols = slice(col, col + group)
            target = labels_ref[:, first + col : first + col + group] - index * tile

            def begin(cols=cols, state=state):
                state.update(
                    own=pick_row(a_ref[:, cols], index),
                    other=pick_row(b_ref[:, cols], index),
                    gap=pick_row(g_ref[:, cols], index),
                    cross=c_ref[:, cols],
                )

            def chunk(start, rows, cols=cols, state=state, target=target):
                here = slice(start, start + rows)
                row = lax.broadcasted_iota(jnp.int32, (rows, group), 0)
                student = ps_ref[here, cols].astype(jnp.float32) * state["own"]
                teacher = pt_ref[here, cols].astype(jnp.float32) * state["other"]
                lowered = l_ref[here, cols].astype(jnp.float32)
                part = teacher * (state["gap"] - lowered)
                value = student - teacher - jnp.where(row == target - start, scale, 0.0)
                state["cross"] = state["cross"] + jnp.sum(part, axis=0, keepdims=True)
                value = value.astype(jnp.bfloat16)
                d_ref[here, cols] = value
                d_refs[slot][here, cols] = value

            def finish(cols=cols, state=state):
                c_ref[:, cols] = state["cross"]

            items.append(begin)
            items += [functools.partial(chunk, start, rows) for start, rows in chunks(valid_rows)]
            items.append(finish)
        return items

    def matmul(slot, start, rows):
        def piece(out):
            def work():
                cols = slice(out, out + PIECE)
                up_ref[:, cols] += lax.dot_general(
                    d_refs[slot][:rows, :], w_ref[pl.ds(start, rows), cols], (((0,), (0,)), ((), ())),
                    preferred_element_type=jnp.float32,
                )

            return work

        return [piece(out) for out in range(0, up_ref.shape[1], PIECE)]

    @pl.when(step == 0)
    def _():
        here = slice(first, first + tokens)
        own_total, other_total = own_ref[0:1, here], other_ref[0:1, here]
        a_ref[...] = jnp.exp(own_ref[8:, here] - own_total) * ((1.0 + BETA) * scale)
        b_ref[...] = jnp.exp(other_ref[8:, here] - other_total) * (BETA * scale)
        g_ref[...] = own_total - own_ref[8:, here]
        c_ref[...] = jnp.zeros_like(c_ref)
        up_ref[...] = jnp.zeros_like(up_ref)
        together([], weigh(0, 0, last_rows if tiles == 1 else tile))

    if tiles > 2:

        for parity in range(2):

            @pl.when((step > 0) & (step < tiles - 1) & (lax.rem(step, 2) == parity))
            def _(parity=parity):
                together(matmul(1 - parity, pl.multiple_of((step - 1) * tile, tile), tile), weigh(parity, step, tile))

    if tiles > 1:

        @pl.when(step == tiles - 1)
        def _():
            together(matmul(tiles % 2, (tiles - 2) * tile, tile), weigh((tiles - 1) % 2, tiles - 1, last_rows))

    @pl.when(step == tiles)
    def _():
        together(matmul((tiles - 1) % 2, (tiles - 1) * tile, last_rows), [])
        width = up_ref.shape[1]
        half = tokens // 2
        column = jnp.broadcast_to(c_ref[...] * (all_tokens / BETA), (LANES, tokens)).T
        lane = lax.broadcasted_iota(jnp.int32, (tokens, LANES), 1)
        if first_ref.dtype == jnp.float32:
            edge = jnp.where(lane == 0, column, 0.0)
        else:
            high = column.astype(jnp.bfloat16).astype(jnp.float32)
            edge = jnp.where(lane == 0, high, jnp.where(lane == 1, column - high, 0.0))
        for ref, place in ((first_ref, 0), (second_ref, half)):
            ref[:, :width] = up_ref[place : place + half, :].astype(ref.dtype)
            ref[:, width:] = edge[place : place + half, :].astype(ref.dtype)


def run_dlogits(group, totals, other_totals, labels, p_own, p_other, lowered, weights, dlogits, out_type):
    tokens = p_own.shape[1]
    vocab_dev, width = weights.shape
    tile, tiles = tiling(vocab_dev, TILE)
    groups = totals.shape[0] - 8
    wide = width + LANES
    ahead = lambda j: jnp.minimum(j, tiles - 1)
    here = pl.BlockSpec((tile, tokens), lambda j: (ahead(j), 0))
    p_own, p_other, lowered = (pltpu.with_memory_space_constraint(v, pltpu.HBM) for v in (p_own, p_other, lowered))
    operands = [totals, other_totals, labels, p_own, p_other, lowered, weights]
    in_specs = [
        whole_vmem(),
        whole_vmem(),
        whole_vmem(),
        here,
        here,
        here,
        pl.BlockSpec(memory_space=pltpu.VMEM),
    ]
    aliases = {}
    if dlogits is not None:
        aliases[len(operands)] = 0
        operands.append(dlogits)
        in_specs.append(pl.BlockSpec(memory_space=pl.ANY))
    return pl.pallas_call(
        functools.partial(dlogits_kernel, tile, tiles, group),
        grid=(tiles + 1,),
        in_specs=in_specs,
        out_specs=[
            pl.BlockSpec((tile, tokens), lambda j: (ahead(j), group)),
            whole_vmem(),
            whole_vmem(),
        ],
        out_shape=[
            jax.ShapeDtypeStruct((vocab_dev, 2 * tokens), jnp.bfloat16),
            jax.ShapeDtypeStruct((tokens // 2, wide), out_type),
            jax.ShapeDtypeStruct((tokens // 2, wide), out_type),
        ],
        scratch_shapes=[
            pltpu.VMEM((tokens, width), jnp.float32),
            pltpu.VMEM((tile, tokens), jnp.bfloat16),
            pltpu.VMEM((tile, tokens), jnp.bfloat16),
            pltpu.VMEM((groups, tokens), jnp.float32),
            pltpu.VMEM((groups, tokens), jnp.float32),
            pltpu.VMEM((groups, tokens), jnp.float32),
            pltpu.VMEM((1, tokens), jnp.float32),
        ],
        input_output_aliases=aliases,
        compiler_params=pltpu.CompilerParams(vmem_limit_bytes=VMEM_SHARED),
        cost_estimate=pl.CostEstimate(
            flops=2 * tokens * width * vocab_dev,
            bytes_accessed=8 * tokens * vocab_dev,
            transcendentals=0,
        ),
        name="dlogits",
    )(*operands)


def fold_kernel(count, gots, sends, *refs):
    sums, arrived, outs = refs[:count], refs[count : count + gots], refs[-1 - sends :]
    keep, send = outs[0], outs[1:]
    width = keep.shape[2] - LANES
    cut = keep.shape[1]
    lane = lax.broadcasted_iota(jnp.int32, (cut, LANES), 1)
    for part in range(2):
        held = sums[part][...] if count == 2 else sums[0][part]
        got = arrived[part][...] if gots == 2 else arrived[0][part]
        total = held + got.astype(jnp.float32)
        keep[part] = total[:cut]
        gone = total[cut:]
        cross = gone[:, width : width + 1] + gone[:, width + 1 : width + 2]
        high = cross.astype(jnp.bfloat16).astype(jnp.float32)
        edge = jnp.where(lane == 0, high, jnp.where(lane == 1, cross - high, 0.0))
        value = jnp.concatenate([gone[:, :width], edge], axis=1).astype(jnp.bfloat16)
        if sends == 2:
            send[part][...] = value
        else:
            send[0][part] = value


def run_fold(sums, arrived, sends, after):
    rows, wide = sums[0].shape[-2:]
    cut = rows // 2
    operands = list(sums) + list(arrived)
    in_specs = [pl.BlockSpec(memory_space=pltpu.VMEM)] * len(operands)
    if after is not None:
        operands.append(pltpu.with_memory_space_constraint(after, pltpu.HBM))
        in_specs.append(pl.BlockSpec(memory_space=pl.ANY))
    shape = (cut, wide) if sends == 2 else (2, cut, wide)
    return pl.pallas_call(
        functools.partial(fold_kernel, len(sums), len(arrived), sends),
        in_specs=in_specs,
        out_specs=[pl.BlockSpec(memory_space=pltpu.VMEM)] * (1 + sends),
        out_shape=[jax.ShapeDtypeStruct((2, cut, wide), jnp.float32)]
        + [jax.ShapeDtypeStruct(shape, jnp.bfloat16)] * sends,
        compiler_params=pltpu.CompilerParams(vmem_limit_bytes=VMEM_SHARED),
        cost_estimate=SMALL,
        name="fold",
    )(*operands)


def finish_kernel(keep_ref, got_ref, rows_ref, gain_ref, base_ref, grad_ref, loss_ref):
    width = rows_ref.shape[1]
    half = keep_ref.shape[1]
    for part in range(2):
        here = slice(part * half, (part + 1) * half)
        total = keep_ref[part] + got_ref[part].astype(jnp.float32)
        values = rows_ref[here, :].astype(jnp.float32)
        inverse = lax.rsqrt(jnp.mean(values * values, axis=-1, keepdims=True) + EPS)
        scaled = gain_ref[...] * total[:, :width]
        inner = jnp.mean(scaled * values, axis=-1, keepdims=True)
        grad_ref[here, :] = (inverse * scaled - values * inverse**3 * inner).astype(grad_ref.dtype)
        cross = total[:, width : width + 1] + total[:, width + 1 : width + 2]
        loss_ref[:, here] = base_ref[:, here] + BETA * jnp.broadcast_to(cross, (half, LANES)).T[0:1, :]


def run_finish(keep, got, rows, gain, base):
    return pl.pallas_call(
        finish_kernel,
        in_specs=[whole_vmem()] * 5,
        out_specs=[whole_vmem()] * 2,
        out_shape=[jax.ShapeDtypeStruct(rows.shape, rows.dtype), jax.ShapeDtypeStruct(base.shape, jnp.float32)],
        compiler_params=pltpu.CompilerParams(vmem_limit_bytes=VMEM_SHARED),
        cost_estimate=SMALL,
        name="finish",
    )(keep, got, rows, gain, base)


def head_grad_kernel(normed_ref, d_ref, *refs):
    out_ref = refs[-1]
    out_ref[...] = jnp.dot(d_ref[...], normed_ref[...], preferred_element_type=jnp.float32).astype(out_ref.dtype)


def run_head_grad(first, count, normed, dlogits, grad, after):
    tokens, width = normed.shape
    vocab_dev = dlogits.shape[0]
    tile, tiles = tiling(vocab_dev, GRAD_TILE)
    operands = [normed, pltpu.with_memory_space_constraint(dlogits, pltpu.HBM)]
    in_specs = [whole((tokens, width)), pl.BlockSpec((tile, tokens), lambda j: (first + j, 0))]
    aliases = {}
    for value in after:
        operands.append(value)
        in_specs.append(pl.BlockSpec(memory_space=pl.ANY))
    if grad is not None:
        aliases[len(operands)] = 0
        operands.append(pltpu.with_memory_space_constraint(grad, pltpu.HBM))
        in_specs.append(pl.BlockSpec(memory_space=pl.ANY))
    return pl.pallas_call(
        head_grad_kernel,
        grid=(count,),
        in_specs=in_specs,
        out_specs=pl.BlockSpec((tile, width), lambda j: (first + j, 0)),
        out_shape=jax.ShapeDtypeStruct((vocab_dev, width), jnp.bfloat16),
        input_output_aliases=aliases,
        compiler_params=pltpu.CompilerParams(vmem_limit_bytes=VMEM_ALONE),
        cost_estimate=pl.CostEstimate(
            flops=2 * tokens * width * tile * count,
            bytes_accessed=2 * width * tile * count + 2 * tokens * tile * count,
            transcendentals=0,
        ),
        name="head_grad",
    )(*operands)


def moved(value, offset):
    n = lax.axis_size("fsdp")
    return lax.ppermute(value, "fsdp", [(i, i ^ offset) for i in range(n)])


def other_member(value):
    return lax.ppermute(value, "member", [(0, 1), (1, 0)])


def token_order(bits):
    offsets = [0]
    for bit in reversed(range(2, bits)):
        offsets = offsets + [o | 1 << bit for o in offsets]
    order = []
    for group in range(2):
        for half in range(2):
            group_bit, place_bit = (1, 2) if half == 0 else (2, 1)
            for place in range(2):
                order += [(group * group_bit + place * place_bit + o, half) for o in offsets]
    return order


def lane_moves(offset, bits, half):
    moves = []
    for bit in range(bits):
        if offset >> bit & 1:
            group, place = half << bits, half << (bits - 2)
            strides = {0: (group, place), 1: (place, group)}.get(bit, (half << (bits - 1 - bit),) * 2)
            moves.append(strides + (half << (bits - 1),))
    return tuple(moves)


def pack(value, width):
    cross = value[..., width : width + 1] + value[..., width + 1 : width + 2]
    high = lax.reduce_precision(cross, 8, 7)
    rest = jnp.zeros(value.shape[:-1] + (LANES - 2,), jnp.float32)
    return jnp.concatenate([value[..., :width], high, cross - high, rest], axis=-1).astype(jnp.bfloat16)


def body(hidden, gain, head, labels):
    own_rows = hidden[0]
    gain_row = gain[0]
    tok_dev, width = own_rows.shape
    vocab_dev = head.shape[2]
    count = lax.axis_size("fsdp")
    bits = count.bit_length() - 1
    index = lax.axis_index("fsdp")
    half = tok_dev // 2
    tokens = tok_dev * count

    order = token_order(bits)
    offsets = jnp.asarray([o for o, _ in order], jnp.int32)
    halves = jnp.asarray([s for _, s in order], jnp.int32)
    local_labels = labels.reshape(2 * count, half)[(offsets ^ index) * 2 + halves].reshape(1, tokens)
    local_labels = local_labels - index * vocab_dev

    first_rows = min(vocab_dev, cdiv(vocab_dev // 2, 16) * 16)
    weights = pinned(run_load(0, first_rows, head[0].T, local_labels, None))
    held = [own_rows]
    for bit in reversed(range(2, bits)):
        held = run_join([held[0], moved(held[0], 1 << bit)], bit == 2, weights)
        if bit == bits - 1 and first_rows < vocab_dev:
            weights = pinned(run_load(first_rows, vocab_dev - first_rows, head[0].T, held[0], weights))
    near_a, near_b = run_stack(weights, held[0], moved(held[0], 2), held[1], moved(held[1], 1))
    far_a = moved(near_a, 1)
    far_b = moved(near_b, 2)

    p_near, l_near, normed, tops, stats = run_logits(
        0, near_a, near_b, gain_row[None], local_labels, weights, []
    )
    p_near_other = other_member(p_near)
    p_far, l_far, normed, tops, table = run_logits(
        1, far_a, far_b, gain_row[None], local_labels, weights, [normed, stats, tops]
    )
    p_far_other = other_member(p_far)

    for bit in range(0, bits, 2):
        steps = [k << bit for k in range(1, 4) if k << bit < count]
        lanes = [lane_moves(k, bits, half) for k in steps]
        table = run_merge(weights, table, [moved(table, k) for k in steps], lanes, tops if bit + 2 >= bits else None)
    other_totals = other_member(table)

    dlogits, send_a, send_b = run_dlogits(
        1, table, other_totals, local_labels, p_far, p_far_other, l_far, weights, None, jnp.bfloat16
    )
    got_a, got_b = moved(send_a, 1), moved(send_b, 2)
    dlogits, sum_a, sum_b = run_dlogits(
        0, table, other_totals, local_labels, p_near, p_near_other, l_near, weights, dlogits, jnp.float32
    )

    tile, tiles = tiling(vocab_dev, GRAD_TILE)
    edges = [tiles * i // 8 for i in GRAD_EDGES]
    grad = None
    summed, sends = run_fold((sum_a, sum_b), (got_a, got_b), 2, None), 2
    for step in range(1, bits):
        keep, send = summed[0], summed[1:]
        if step <= 3 and edges[step] > edges[step - 1]:
            grad = run_head_grad(edges[step - 1], edges[step] - edges[step - 1], normed, dlogits, grad, send)
        if step == 1:
            got = [moved(send[0], 2), moved(send[1], 1)]
        else:
            got = [moved(send[0], 1 << step)]
        if step == bits - 1 and half % 16 == 0:
            break
        cut = keep.shape[1] // 2
        if step < bits - 1 and cut % 16 == 0:
            summed = run_fold((keep,), got, 1, grad)
        else:
            total = keep + (jnp.stack(got) if step == 1 else got[0]).astype(jnp.float32)
            if step < bits - 1:
                summed = [total[:, :cut], pack(total[:, cut:], width)]
            else:
                summed = total
    quarter = tokens // 4
    own = lambda row: jnp.concatenate([row[:half], row[quarter : quarter + half]])
    base = own(table[0]) - own(table[1])
    if half % 16 == 0:
        hidden_grad, token_loss = run_finish(keep, got[0], own_rows, gain_row[None], base[None])
        return (token_loss, grad.T[None], hidden_grad[None])
    summed = summed.reshape(tok_dev, -1)
    cross = summed[:, width] + summed[:, width + 1]
    summed = summed[:, :width]

    token_loss = base + BETA * cross
    values = own_rows.astype(jnp.float32)
    inverse = lax.rsqrt(jnp.mean(values * values, axis=-1, keepdims=True) + EPS)
    scaled = gain_row * summed
    inner = jnp.mean(scaled * values, axis=-1, keepdims=True)
    hidden_grad = inverse * scaled - values * inverse**3 * inner
    return (token_loss[None], grad.T[None], hidden_grad.astype(jnp.bfloat16)[None])


def solution(mesh):
    in_specs = (P("member", "fsdp", None), P("member", None), P("member", None, "fsdp"), P())
    out_specs = (P("member", "fsdp"), P("member", None, "fsdp"), P("member", "fsdp", None))
    return jax.shard_map(body, mesh=mesh, in_specs=in_specs, out_specs=out_specs, check_vma=False)
```
